128 devices in a mesh: dp: 8 (over y, z_lo), tensor: 16 (over z_hi, x, core).
Axes of the slice: x: 4, y: 4, z: 4 (z_hi: 2, z_lo: 2; z = z_hi * 2 + z_lo), core: 2. Of those that a mesh axis runs over, the one named last changes fastest.
Arguments:
- tokens: bfloat16 [12288, 5120], P(('dp', 'tensor')), may hold values from -6 to 6
- codes: bfloat16 [128, 5120, 128], P(('dp', 'tensor')), may hold values from -4 to 4
- block_ids: int32 [128], P(('dp', 'tensor')), may hold values from 0 to 7, as said below
- scale_idx: int32 [128], P(('dp', 'tensor')), may hold values from 0 to 63
- scale_table: float32 [64], replicated, may hold values from 0.006 to 0.03
- down_weight: bfloat16 [8192, 5120], P('tensor'), may hold values from -0.0625 to 0.0625
Outputs:
- mixed: bfloat16 [12288, 5120], P(('dp', 'tensor'))
The draws below stay inside these ranges and needn't reach their ends.
Inputs may be any that keep to these rules, and one draw needn't show every extreme that they name: `block_ids`: the 8 slots that belong to one tensor rank hold each local column block number exactly once.
All inputs are finite; a program needn't handle non-finite values.
Results may differ from the reference program's by a relative error of at most 0.018.
Values may be sent and summed in bfloat16 or wider, within the bound.
No kernel may reach another device: no remote copies, remote signals or barrier semaphores. Data moves between devices by JAX's collectives and lax.ppermute only.
A program may use at most 128 MiB of HBM per device.

```python
import math
import jax
import jax.numpy as jnp
from jax import lax

D = 5120
FF = 8192
BW = 128
NSCALE = 64
TOKENS = 12288
NBLK = 128
N_DP = 8
N_TENSOR = 16


def draw_block_ids(key, part):
    key = jax.random.fold_in(key, 7)
    slots = 2 * FF // (N_TENSOR * BW)
    keys = jax.random.split(key, N_TENSOR)
    perms = jax.vmap(lambda k: jax.random.permutation(k, slots))(keys)
    return perms.reshape(N_TENSOR, N_DP, slots // N_DP).transpose(1, 0, 2).reshape(-1).astype(jnp.int32)


def place_ends(entries, stream_key, smallest, top_value):
    extent = entries.shape
    place = [jax.random.randint(jax.random.fold_in(stream_key, axis), (), 0, extent[axis]) for axis in range(len(extent))]
    entries = entries.at[tuple(place)].set(smallest)
    longest = extent.index(max(extent))
    place[longest] = (place[longest] + 1) % extent[longest]
    return entries.at[tuple(place)].set(top_value)


def levels(own_key, shape, cuts, least, largest):
    level = 1.0
    for axis_at, shards_of in cuts:
        draws = jax.random.uniform(jax.random.fold_in(jax.random.fold_in(own_key, 6), axis_at), (shards_of,), jnp.float32, least / len(cuts), largest / len(cuts))
        level = level * jnp.repeat(jnp.exp(draws), shape[axis_at] // shards_of).reshape((-1,) + (1,) * (len(shape) - 1 - axis_at))
    return level


def gaussian(stream_key, shape, scale, limit, cuts=(), held_as=jnp.bfloat16):
    entries = scale * jax.random.normal(stream_key, shape, jnp.float32)
    if cuts:
        entries = entries * levels(stream_key, shape, cuts, -0.22, 0.18)
    return jnp.clip(entries, -limit, limit).astype(held_as)


def setup_inputs(seed: int = 0) -> dict:
    splits = jax.random.split(jax.random.key(seed), 7)
    tokens = gaussian(splits[0], (TOKENS, D), 1.0, 6.0, ((0, 128),))
    codes = gaussian(splits[1], (NBLK, D, BW), 1.0, 4.0, ((0, 128),))
    block_ids = draw_block_ids(jax.random.fold_in(splits[6], 71), 0)
    scale_idx = place_ends(jax.random.randint(splits[3], (NBLK,), 0, NSCALE), jax.random.fold_in(splits[3], 1), 0, NSCALE - 1).astype(jnp.int32)
    scale_table = jnp.clip(jnp.exp(jax.random.uniform(splits[4], (NSCALE,), jnp.float32, math.log(0.006), math.log(0.03))), 0.006, 0.03)
    down_weight = gaussian(splits[5], (FF, D), FF ** -0.5, 0.0625, ((0, 16),))
    return dict(tokens=tokens, codes=codes, block_ids=block_ids, scale_idx=scale_idx, scale_table=scale_table, down_weight=down_weight)


def reference(tokens, codes, block_ids, scale_idx, scale_table, down_weight):
    slots = 2 * FF // (N_TENSOR * BW)
    per_dev = slots // N_DP
    codes_r = codes.reshape(N_DP, N_TENSOR, per_dev, D, BW).transpose(1, 0, 2, 3, 4).reshape(N_TENSOR, slots, D, BW)
    ids_r = block_ids.reshape(N_DP, N_TENSOR, per_dev).transpose(1, 0, 2).reshape(N_TENSOR, slots)
    sidx_r = scale_idx.reshape(N_DP, N_TENSOR, per_dev).transpose(1, 0, 2).reshape(N_TENSOR, slots)
    local_ff = FF // N_TENSOR
    down_r = down_weight.reshape(N_TENSOR, local_ff, D)
    tokens_wide = tokens.astype(jnp.float32)

    def one_rank(carry, inputs):
        block_codes, block_nums, block_sidx, down_part = inputs
        order = jnp.argsort(block_nums)
        ordered = block_codes[order].astype(jnp.float32)
        scales = scale_table[block_sidx[order]]
        proj = jnp.einsum('rd,gdb->rgb', tokens_wide, ordered) * scales[None, :, None]
        proj = proj.reshape(proj.shape[0], 2, local_ff)
        hidden = (jax.nn.silu(proj[:, 0]) * proj[:, 1]).astype(jnp.bfloat16)
        partial_t = jnp.dot(hidden, down_part, preferred_element_type=jnp.float32).astype(jnp.bfloat16)
        partial_t = lax.optimization_barrier(partial_t)
        return carry + partial_t.astype(jnp.float32), None

    start = jnp.zeros((tokens.shape[0], D), jnp.float32)
    total, _ = lax.scan(one_rank, start, (codes_r, ids_r, sidx_r, down_r))
    return total.astype(jnp.bfloat16)
```

```python
import jax
import jax.numpy as jnp
from jax import lax
from jax.sharding import PartitionSpec as P

NX, NY, NZL, NZH, NC = 4, 4, 2, 2, 2
AXES = ("dp", "tensor")


def place(y, zl, zh, x, c):
    return ((y % NY * NZL + zl % NZL) * NZH + zh % NZH) * NX * NC + x % NX * NC + c % NC


def move(value, dx=0, dy=0, zl=0, zh=0, core=0):
    pairs = []
    for y in range(NY):
        for l in range(NZL):
            for h in range(NZH):
                for x in range(NX):
                    for c in range(NC):
                        pairs.append((place(y, l, h, x, c), place(y + dy, l + zl, h + zh, x + dx, c + core)))
    return lax.ppermute(value, AXES, pairs)


def rows_of(*parts):
    return jnp.concatenate(parts, axis=0)


def gather_small(block_ids, scale_idx):
    both = jnp.stack([block_ids[0], scale_idx[0]])
    wide = jnp.broadcast_to(both[:, None], (2, 128)).reshape(1, 256)
    every = lax.all_gather(wide, "dp", axis=0, tiled=True)
    return every[:, 0], every[:, 128]


def dot32(a, b):
    return jnp.dot(a, b, preferred_element_type=jnp.float32)


def body(tokens, codes, block_ids, scale_idx, scale_table, down_weight):
    half_rows = tokens.shape[0] // 2
    count = tokens.shape[0]
    depth = tokens.shape[1]
    half_depth = depth // 2
    bf16 = jnp.bfloat16

    own = codes[0]
    code = {(0, 0): own}
    tok = {(0, 0): tokens}
    code[0, 1] = move(own, zl=1)
    tok[0, 1] = move(tokens, zh=1)
    for p in (0, 1):
        code[-1, p] = move(code[0, p], dy=1)
        code[1, p] = move(code[0, p], dy=-1)
        tok[-1, p] = move(tok[0, p], dx=1)
        tok[1, p] = move(tok[0, p], dx=-1)
    for p in (0, 1):
        code[2, p] = rows_of(
            move(code[-1, p][:half_depth], dy=1), move(code[1, p][half_depth:], dy=-1)
        )
        tok[2, p] = rows_of(
            move(tok[-1, p][:half_rows], dx=1), move(tok[1, p][half_rows:], dx=-1)
        )
    order_of_rows = ((2, 0), (2, 1), (1, 1), (-1, 1), (1, 0), (-1, 0), (0, 1), (0, 0))
    other = {}
    for pair in (((0, 1), (0, 0)), ((1, 0), (-1, 0)), ((1, 1), (-1, 1)), ((2, 0), (2, 1))):
        got = move(rows_of(tok[pair[0]], tok[pair[1]]), core=1)
        other[pair[0]], other[pair[1]] = got[:count], got[count:]
    rows = rows_of(*[r for k in order_of_rows for r in (tok[k], other[k])])

    me = lax.axis_index("dp")
    y, l = me // NZL, me % NZL
    slots = ((0, 0), (0, 1), (-1, 0), (1, 0), (-1, 1), (1, 1), (2, 0), (2, 1))
    dp_of = jnp.stack([((y + d) % NY) * NZL + (l + p) % NZL for d, p in slots])
    ids, sidx = gather_small(block_ids, scale_idx)
    ids, sidx = ids[dp_of], sidx[dp_of]
    scales = jnp.sum(
        jnp.where(sidx[:, None] == jnp.arange(scale_table.shape[0])[None, :], scale_table[None, :], 0.0), axis=1
    )
    proj = []
    for i in range(0, len(slots), 2):
        pair = jnp.stack([code[slots[i]], code[slots[i + 1]]])
        proj.append(jnp.einsum("rd,gdb->grb", rows, pair, preferred_element_type=jnp.float32))
    proj = jnp.concatenate(proj, axis=0) * scales[:, None, None]
    slot_at = jnp.argsort(ids)
    hidden = []
    for b in range(4):
        gate = lax.dynamic_index_in_dim(proj, slot_at[b], 0, keepdims=False)
        up = lax.dynamic_index_in_dim(proj, slot_at[b + 4], 0, keepdims=False)
        hidden.append((jax.nn.silu(gate) * up).astype(bf16))
    hidden = jnp.concatenate(hidden, axis=1)

    total = {}
    for pair in (((2, 0), (2, 1)), ((1, 1), (-1, 1)), ((1, 0), (-1, 0)), ((0, 1), (0, 0))):
        first = order_of_rows.index(pair[0]) * 2 * count
        part = dot32(hidden[first : first + 4 * count], down_weight)
        part = part.reshape(2, 2, count, depth)
        got = move(part[:, 1].astype(bf16).reshape(2 * count, depth), core=1).reshape(2, count, depth)
        both = part[:, 0].astype(bf16).astype(jnp.float32) + got.astype(jnp.float32)
        total[pair[0]], total[pair[1]] = both[0], both[1]
    top = move(rows_of(total[2, 0][:half_rows], total[2, 1][:half_rows]).astype(bf16), dx=1)
    low = move(rows_of(total[2, 0][half_rows:], total[2, 1][half_rows:]).astype(bf16), dx=-1)
    result = {}
    for p in (1, 0):
        add_top = top[p * half_rows : (p + 1) * half_rows].astype(jnp.float32)
        add_low = low[p * half_rows : (p + 1) * half_rows].astype(jnp.float32)
        right = rows_of(total[1, p][:half_rows] + add_top, total[1, p][half_rows:]).astype(bf16)
        left = rows_of(total[-1, p][:half_rows], total[-1, p][half_rows:] + add_low).astype(bf16)
        right = move(right, dx=1).astype(jnp.float32)
        left = move(left, dx=-1).astype(jnp.float32)
        result[p] = total[0, p] + right + left
    last = move(result[1].astype(bf16), zh=1)
    return (result[0] + last.astype(jnp.float32)).astype(bf16)


def solution(mesh):
    return jax.shard_map(
        body,
        mesh=mesh,
        in_specs=(
            P(("dp", "tensor"), None),
            P(("dp", "tensor"), None, None),
            P(("dp", "tensor")),
            P(("dp", "tensor")),
            P(),
            P("tensor", None),
        ),
        out_specs=P(("dp", "tensor"), None),
        check_vma=False,
    )
```

```python
import jax
import jax.numpy as jnp
from jax import lax
from jax.experimental import pallas as pl
from jax.experimental.pallas import tpu as pltpu
from jax.sharding import PartitionSpec as P

NX, NY, NZL, NZH, NC = 4, 4, 2, 2, 2
AXES = ("dp", "tensor")
BF16, F32 = jnp.bfloat16, jnp.float32
NOTE = 16


def place(y, zl, zh, x, c):
    return ((y % NY * NZL + zl % NZL) * NZH + zh % NZH) * NX * NC + x % NX * NC + c % NC


def move(value, dx=0, dy=0, zl=0, zh=0, core=0):
    pairs = []
    for y in range(NY):
        for l in range(NZL):
            for h in range(NZH):
                for x in range(NX):
                    for c in range(NC):
                        pairs.append((place(y, l, h, x, c), place(y + dy, l + zl, h + zh, x + dx, c + core)))
    return lax.ppermute(value, AXES, pairs)


def rows_of(*parts):
    return jnp.concatenate(parts, axis=0)


def feed_forward(code_map, n_codes, row_counts, depth, width, local_ff):
    slots = len({m[0] for m in code_map})
    blocks = slots // 2
    rows = sum(row_counts)
    n_copies = len(code_map) + len(row_counts) + 1

    def kernel(ids, sidx, table, *refs):
        sources, refs = refs[:n_codes], refs[n_codes:]
        pieces, refs = refs[: len(row_counts)], refs[len(row_counts) :]
        down, mine, sibling, w, x, dn, proj, hid, sem = refs
        copies = []
        at = 0
        x_copies = []
        for i, n in enumerate(row_counts):
            x_copies.append(pltpu.make_async_copy(pieces[i], x.at[pl.ds(at, n)], sem.at[len(copies) + i]))
            at += n
        base = len(x_copies)
        code_copies = []
        for i, (slot, src, first, n, dst) in enumerate(code_map):
            target = w.at[slot // 2, pl.ds(dst, n), pl.ds(slot % 2 * width, width)]
            code_copies.append(
                pltpu.make_async_copy(sources[src].at[pl.ds(first, n)], target, sem.at[base + i])
            )
        down_copy = pltpu.make_async_copy(down, dn, sem.at[n_copies - 1])
        for c in x_copies + code_copies + [down_copy]:
            c.start()
        for c in x_copies:
            c.wait()
        for pair in range(blocks):
            for m, c in zip(code_map, code_copies):
                if m[0] // 2 == pair:
                    c.wait()
            acc = jnp.dot(x[...], w[pair], preferred_element_type=F32)
            for side in range(2):
                slot = 2 * pair + side
                proj[ids[slot]] = acc[:, side * width : (side + 1) * width] * table[sidx[slot]]
        for b in range(blocks):
            gate, up = proj[b], proj[b + blocks]
            hid[:, b * width : (b + 1) * width] = (gate / (1.0 + jnp.exp(-gate)) * up).astype(BF16)
        down_copy.wait()
        step = 1024
        for n in range(depth // step):
            out = jnp.dot(hid[...], dn[:, n * step : (n + 1) * step], preferred_element_type=F32).astype(BF16)
            mine[:, n * step : (n + 1) * step] = out[: rows // 2]
            sibling[:, n * step : (n + 1) * step] = out[rows // 2 :]

    any_spec = pl.BlockSpec(memory_space=pl.ANY)
    smem = pl.BlockSpec(memory_space=pltpu.SMEM)
    vmem = pl.BlockSpec(memory_space=pltpu.VMEM)
    half = jax.ShapeDtypeStruct((rows // 2, depth), BF16)
    return pl.pallas_call(
        kernel,
        out_shape=(half, half),
        in_specs=[smem] * 3 + [any_spec] * (n_codes + len(row_counts) + 1),
        out_specs=(vmem, vmem),
        scratch_shapes=[
            pltpu.VMEM((blocks, depth, 2 * width), BF16),
            pltpu.VMEM((rows, depth), BF16),
            pltpu.VMEM((local_ff, depth), BF16),
            pltpu.VMEM((slots, rows, width), F32),
            pltpu.VMEM((rows, local_ff), BF16),
            pltpu.SemaphoreType.DMA((n_copies,)),
        ],
        compiler_params=pltpu.CompilerParams(vmem_limit_bytes=44 * 2**20),
        cost_estimate=pl.CostEstimate(
            flops=2 * rows * depth * local_ff * 3,
            bytes_accessed=2 * (depth * slots * width + local_ff * depth + 2 * rows * depth),
            transcendentals=rows * local_ff,
        ),
    )


def body(tokens, codes, block_ids, scale_idx, scale_table, down_weight):
    count, depth = tokens.shape
    width = codes.shape[2]
    local_ff = down_weight.shape[0]
    h_rows, h_depth = count // 2, depth // 2

    line = lax.broadcasted_iota(jnp.int32, (NOTE, width), 0)
    note = jnp.where(line == 0, block_ids[0], scale_idx[0]).astype(BF16)
    own = rows_of(codes[0], note)

    cz = move(own, zl=1)
    ca, cb = move(own, dy=1), move(own, dy=-1)
    caz, cbz = move(cz, dy=1), move(cz, dy=-1)
    c_top = move(rows_of(ca[:h_depth], caz[:h_depth], ca[depth:], caz[depth:]), dy=1)
    c_low = move(rows_of(cb[h_depth:depth], cbz[h_depth:depth]), dy=-1)
    sources = [own, cz, ca, cb, caz, cbz, c_top, c_low]
    code_map = [(i, i, 0, depth, 0) for i in range(6)]
    for i in range(2):
        code_map += [(6 + i, 6, i * h_depth, h_depth, 0), (6 + i, 7, i * h_depth, h_depth, h_depth)]
    notes = jnp.stack([s[depth : depth + 2, 0] for s in sources[:6]] + [c_top[depth + i * NOTE : depth + i * NOTE + 2, 0] for i in range(2)])
    notes = notes.astype(jnp.int32)
    ids, sidx = notes[:, 0], notes[:, 1]

    tz = move(tokens, zh=1)
    ta, tb = move(tokens, dx=1), move(tokens, dx=-1)
    taz, tbz = move(tz, dx=1), move(tz, dx=-1)
    t_top = move(rows_of(ta[:h_rows], taz[:h_rows]), dx=1)
    t_low = move(rows_of(tb[h_rows:], tbz[h_rows:]), dx=-1)

    run = feed_forward(code_map, len(sources), (count, count, 2 * count), depth, width, local_ff)

    def sums(first, second):
        other = move(rows_of(first, second), core=1)
        mine, sibling = run(ids, sidx, scale_table, *sources, first, second, other, down_weight)
        got = move(sibling, core=1)
        return mine.astype(F32) + got.astype(F32)

    far = sums(t_top, t_low)
    top = move(far[:count].astype(BF16), dx=1).astype(F32)
    low = move(far[count:].astype(BF16), dx=-1).astype(F32)
    sides = {1: sums(tbz, taz), 0: sums(tb, ta)}
    here = sums(tz, tokens)
    result = {}
    for p in (1, 0):
        right, left = sides[p][:count], sides[p][count:]
        right = rows_of(right[:h_rows] + top[p * h_rows : (p + 1) * h_rows], right[h_rows:])
        left = rows_of(left[:h_rows], left[h_rows:] + low[p * h_rows : (p + 1) * h_rows])
        result[p] = move(right.astype(BF16), dx=1).astype(F32) + move(left.astype(BF16), dx=-1).astype(F32)
    last = move((here[:count] + result[1]).astype(BF16), zh=1)
    return (here[count:] + result[0] + last.astype(F32)).astype(BF16)


def solution(mesh):
    return jax.shard_map(
        body,
        mesh=mesh,
        in_specs=(
            P(("dp", "tensor"), None),
            P(("dp", "tensor"), None, None),
            P(("dp", "tensor")),
            P(("dp", "tensor")),
            P(),
            P("tensor", None),
        ),
        out_specs=P(("dp", "tensor"), None),
        check_vma=False,
    )
```

```python
import jax
import jax.numpy as jnp
from jax import lax
from jax.experimental import pallas as pl
from jax.experimental.pallas import tpu as pltpu
from jax.sharding import PartitionSpec as P

NX, NY, NZL, NZH, NC = 4, 4, 2, 2, 2
AXES = ("dp", "tensor")
BF16, F32 = jnp.bfloat16, jnp.float32
NOTE = 16
STEP = 1024


def place(y, zl, zh, x, c):
    return ((y % NY * NZL + zl % NZL) * NZH + zh % NZH) * NX * NC + x % NX * NC + c % NC


def move(value, dx=0, dy=0, zl=0, zh=0, core=0):
    pairs = []
    for y in range(NY):
        for l in range(NZL):
            for h in range(NZH):
                for x in range(NX):
                    for c in range(NC):
                        pairs.append((place(y, l, h, x, c), place(y + dy, l + zl, h + zh, x + dx, c + core)))
    return lax.ppermute(value, AXES, pairs)


def after(value, *others):
    return lax.optimization_barrier((value,) + others)[0]


def rows_of(*parts):
    return jnp.concatenate(parts, axis=0)


def with_note(codes, block_ids, scale_idx):
    _, depth, width = codes.shape

    def kernel(number, entry, block, out, note, sem):
        big = pltpu.make_async_copy(block.at[0], out.at[pl.ds(0, depth)], sem.at[0])
        big.start()
        line = lax.broadcasted_iota(jnp.int32, (NOTE, width), 0)
        note[...] = jnp.where(line == 0, number[0], entry[0]).astype(F32).astype(BF16)
        small = pltpu.make_async_copy(note, out.at[pl.ds(depth, NOTE)], sem.at[1])
        small.start()
        small.wait()
        big.wait()

    smem = pl.BlockSpec(memory_space=pltpu.SMEM)
    anywhere = pl.BlockSpec(memory_space=pltpu.HBM)
    return pl.pallas_call(
        kernel,
        out_shape=jax.ShapeDtypeStruct((depth + NOTE, width), BF16),
        in_specs=[smem, smem, anywhere],
        out_specs=anywhere,
        scratch_shapes=[pltpu.VMEM((NOTE, width), BF16), pltpu.SemaphoreType.DMA((2,))],
        compiler_params=pltpu.CompilerParams(vmem_limit_bytes=2 * 2**20),
    )(block_ids, scale_idx, codes)


def feed_forward(code_map, row_map, depth, width, local_ff, parts):
    n_codes = 1 + max(m[1] for m in code_map)
    n_rows = 1 + max(m[0] for m in row_map)
    slots = 1 + max(m[0] for m in code_map)
    blocks = slots // 2
    rows = sum(m[2] for m in row_map)
    n_copies = len(code_map) + len(row_map) + 1 + 2 * (1 + parts)
    base = len(code_map) + len(row_map)

    def kernel(ids, sidx, table, *refs):
        sources, refs = refs[:n_codes], refs[n_codes:]
        pieces, refs = refs[:n_rows], refs[n_rows:]
        down, outs, (w, x, dn, proj, hid, out, sem) = refs[0], refs[1 : 2 + parts], refs[2 + parts :]
        at = 0
        first = []
        for i, (src, start, n) in enumerate(row_map):
            first.append(pltpu.make_async_copy(pieces[src].at[pl.ds(start, n)], x.at[pl.ds(at, n)], sem.at[i]))
            at += n
        x_copies = list(first)
        waits = [[] for _ in range(blocks)]
        for i, (slot, src, start, n, to) in enumerate(code_map):
            target = w.at[slot // 2, pl.ds(to, n), pl.ds(slot % 2 * width, width)]
            waits[slot // 2].append(
                pltpu.make_async_copy(sources[src].at[pl.ds(start, n)], target, sem.at[len(row_map) + i])
            )
        down_copy = pltpu.make_async_copy(down, dn, sem.at[n_copies - 1])
        stages = [first + waits[0]] + waits[1:] + [[down_copy]]
        for stage in stages[:2]:
            for c in stage:
                c.start()
        for c in x_copies:
            c.wait()

        @pl.loop(0, blocks)
        def _(pair):
            for q in range(blocks):

                @pl.when(pair == q)
                def _(q=q):
                    for c in waits[q]:
                        c.wait()
                    if q + 2 < len(stages):
                        for c in stages[q + 2]:
                            c.start()

            acc = jnp.dot(x[...], w[pair], preferred_element_type=F32)
            for side in range(2):
                slot = 2 * pair + side
                proj[ids[slot]] = acc[:, side * width : (side + 1) * width] * table[sidx[slot]]

        for b in range(blocks):
            gate, up = proj[b], proj[b + blocks]
            hid[:, b * width : (b + 1) * width] = (gate / (1.0 + jnp.exp(-gate)) * up).astype(BF16)
        down_copy.wait()

        def leave(n, slot):
            cols = pl.ds(pl.multiple_of(n * STEP, STEP), STEP)
            piece = rows // 2 // parts
            ranges = [(0, rows // 2)] + [(rows // 2 + i * piece, piece) for i in range(parts)]
            return [
                pltpu.make_async_copy(
                    out.at[slot, pl.ds(at, n)], outs[i].at[:, cols], sem.at[base + slot * (1 + parts) + i]
                )
                for i, (at, n) in enumerate(ranges)
            ]

        steps = depth // STEP

        @pl.loop(0, steps)
        def _(n):
            slot = lax.rem(n, 2)

            @pl.when(n >= 2)
            def _():
                for c in leave(n - 2, slot):
                    c.wait()

            cols = pl.ds(pl.multiple_of(n * STEP, STEP), STEP)
            out[slot] = jnp.dot(hid[...], dn[:, cols], preferred_element_type=F32).astype(BF16)
            for c in leave(n, slot):
                c.start()

        for n in (steps - 2, steps - 1):
            for c in leave(n, n % 2):
                c.wait()

    anywhere = pl.BlockSpec(memory_space=pltpu.HBM)
    smem = pl.BlockSpec(memory_space=pltpu.SMEM)
    half = jax.ShapeDtypeStruct((rows // 2, depth), BF16)
    piece = jax.ShapeDtypeStruct((rows // 2 // parts, depth), BF16)
    return pl.pallas_call(
        kernel,
        out_shape=(half,) + (piece,) * parts,
        in_specs=[smem] * 3 + [anywhere] * (n_codes + n_rows + 1),
        out_specs=(anywhere,) * (1 + parts),
        scratch_shapes=[
            pltpu.VMEM((blocks, depth, 2 * width), BF16),
            pltpu.VMEM((rows, depth), BF16),
            pltpu.VMEM((local_ff, depth), BF16),
            pltpu.VMEM((slots, rows, width), F32),
            pltpu.VMEM((rows, local_ff), BF16),
            pltpu.VMEM((2, rows, STEP), BF16),
            pltpu.SemaphoreType.DMA((n_copies,)),
        ],
        compiler_params=pltpu.CompilerParams(vmem_limit_bytes=60 * 2**20),
        cost_estimate=pl.CostEstimate(
            flops=2 * rows * depth * local_ff * 3,
            bytes_accessed=2 * (depth * slots * width + local_ff * depth + 2 * rows * depth),
            transcendentals=rows * local_ff,
        ),
    )


def body(tokens, codes, block_ids, scale_idx, scale_table, down_weight):
    count, depth = tokens.shape
    width = codes.shape[2]
    local_ff = down_weight.shape[0]
    h_rows, h_depth = count // 2, depth // 2

    own = with_note(codes, block_ids, scale_idx)
    ca, cb = move(own, dy=1), move(own, dy=-1)
    ta, tb, tz = move(tokens, dx=1), move(tokens, dx=-1), move(tokens, zh=1)
    cz = move(after(own, tz), zl=1)
    y_top = move(rows_of(ca[:h_depth], ca[depth:]), dy=1)
    y_low = move(cb[h_depth:depth], dy=-1)
    taz, tbz = move(tz, dx=1), move(tz, dx=-1)
    cy = rows_of(y_top[:h_depth], y_low, y_top[h_depth:])
    caz, cbz, cyz = move(cz, dy=1), move(cz, dy=-1), move(cy, zl=1)
    x_top = move(rows_of(ta[:h_rows], taz[:h_rows]), dx=1)
    x_low = move(rows_of(tb[h_rows:], tbz[h_rows:]), dx=-1)

    sources = [own, ca, cb, cz, cy, caz, cbz, cyz]
    code_map = [(i, i, 0, depth, 0) for i in range(8)]
    notes = jnp.stack([s[depth : depth + 2, 0] for s in sources]).astype(jnp.int32)
    ids, sidx = notes[:, 0], notes[:, 1]

    def swap(*pieces):
        return [move(piece, core=1) for piece in pieces]

    def sums(ids, pieces, parts=3):
        run = feed_forward(code_map, [(i, 0, count) for i in range(4)], depth, width, local_ff, parts)
        return tuple(run(ids, sidx, scale_table, *sources, *pieces, down_weight))

    def add(mine, siblings):
        return mine.astype(F32) + rows_of(*siblings).astype(F32)

    def towards(p, both, top, low):
        top, low = (v[p * h_rows : (p + 1) * h_rows].astype(F32) for v in (top, low))
        right, left = both[:count], both[count:]
        right = rows_of(right[:h_rows] + top, right[h_rows:])
        left = rows_of(left[:h_rows], left[h_rows:] + low)
        return right.astype(BF16), left.astype(BF16)

    x_top, x_low = after((x_top, x_low), caz, cbz, cyz)
    o_far = swap(x_top, x_low)
    later = after((tbz, taz, tb, ta, tz, tokens), *o_far)
    o_near_z, o_near, o_here = swap(*later[:2]), swap(*later[2:4]), swap(*later[4:])
    far = sums(ids, (x_top, x_low, *o_far))
    far = after(far, *o_near_z, *o_near, *o_here)
    far = add(far[0], swap(*far[1:]))
    far_top, far_low = far[:count].astype(BF16), far[count:].astype(BF16)
    top, low = move(far_top, dx=1), move(far_low, dx=-1)

    ids = after(ids, far_top, far_low)
    near_z = sums(ids, (tbz, taz, *o_near_z))
    ids = after(ids, near_z[0])
    here = sums(ids, (tz, tokens, *o_here), 1)
    near_z, top, low, here = after((near_z[:1] + tuple(swap(*near_z[1:])), top, low, here))
    right, left = towards(1, add(near_z[0], near_z[1:]), top, low)
    z_right, z_left = move(right, dx=1), move(left, dx=-1)

    o_sums = swap(after(here[1], right, left))
    ids = after(ids, right, left, *o_sums)
    near = sums(ids, (tb, ta, *o_near))
    near, z_right, z_left = after((near[:1] + tuple(swap(*near[1:])), z_right, z_left))
    right, left = towards(0, add(near[0], near[1:]), top, low)
    here = add(here[0], o_sums)
    across = (here[:count] + z_right.astype(F32) + z_left.astype(F32)).astype(BF16)
    right, left, across = move(right, dx=1), move(left, dx=-1), move(across, zh=1)
    return (here[count:] + right.astype(F32) + left.astype(F32) + across.astype(F32)).astype(BF16)


def solution(mesh):
    return jax.shard_map(
        body,
        mesh=mesh,
        in_specs=(
            P(("dp", "tensor"), None),
            P(("dp", "tensor"), None, None),
            P(("dp", "tensor")),
            P(("dp", "tensor")),
            P(),
            P("tensor", None),
        ),
        out_specs=P(("dp", "tensor"), None),
        check_vma=False,
    )
```

```python
import jax
import jax.numpy as jnp
from jax import lax
from jax.experimental import pallas as pl
from jax.experimental.pallas import tpu as pltpu
from jax.sharding import PartitionSpec as P

NX, NY, NZL, NZH, NC = 4, 4, 2, 2, 2
AXES = ("dp", "tensor")
BF16, F32 = jnp.bfloat16, jnp.float32
NOTE = 16
STEP = 1024


def place(y, zl, zh, x, c):
    return ((y % NY * NZL + zl % NZL) * NZH + zh % NZH) * NX * NC + x % NX * NC + c % NC


def move(value, dx=0, dy=0, zl=0, zh=0, core=0):
    pairs = []
    for y in range(NY):
        for l in range(NZL):
            for h in range(NZH):
                for x in range(NX):
                    for c in range(NC):
                        pairs.append((place(y, l, h, x, c), place(y + dy, l + zl, h + zh, x + dx, c + core)))
    return lax.ppermute(value, AXES, pairs)


def after(value, *others):
    return lax.optimization_barrier((value,) + others)[0]


def rows_of(*parts):
    return jnp.concatenate(parts, axis=0)


def with_note(codes, block_ids, scale_idx):
    _, depth, width = codes.shape

    def kernel(number, entry, block, out, note, sem):
        big = pltpu.make_async_copy(block.at[0], out.at[pl.ds(0, depth)], sem.at[0])
        big.start()
        line = lax.broadcasted_iota(jnp.int32, (NOTE, width), 0)
        note[...] = jnp.where(line == 0, number[0], entry[0]).astype(F32).astype(BF16)
        small = pltpu.make_async_copy(note, out.at[pl.ds(depth, NOTE)], sem.at[1])
        small.start()
        small.wait()
        big.wait()

    smem = pl.BlockSpec(memory_space=pltpu.SMEM)
    anywhere = pl.BlockSpec(memory_space=pltpu.HBM)
    return pl.pallas_call(
        kernel,
        out_shape=jax.ShapeDtypeStruct((depth + NOTE, width), BF16),
        in_specs=[smem, smem, anywhere],
        out_specs=anywhere,
        scratch_shapes=[pltpu.VMEM((NOTE, width), BF16), pltpu.SemaphoreType.DMA((2,))],
        compiler_params=pltpu.CompilerParams(vmem_limit_bytes=2 * 2**20),
    )(block_ids, scale_idx, codes)


def feed_forward(code_map, row_map, ranges, depth, width, local_ff):
    n_codes = 1 + max(m[1] for m in code_map)
    n_rows = 1 + max(m[0] for m in row_map)
    slots = 1 + max(m[0] for m in code_map)
    blocks = slots // 2
    rows = sum(m[2] for m in row_map)
    tile = rows if rows <= 576 else rows // 2
    n_out = len(ranges)
    base = len(code_map) + len(row_map)
    n_copies = base + 1 + 2 * n_out

    def kernel(ids, sidx, table, *refs):
        sources, refs = refs[:n_codes], refs[n_codes:]
        pieces, refs = refs[:n_rows], refs[n_rows:]
        down, outs, (w, x, dn, proj, hid, out, sem) = refs[0], refs[1 : 1 + n_out], refs[1 + n_out :]
        at = 0
        first = []
        for i, (src, start, n) in enumerate(row_map):
            first.append(pltpu.make_async_copy(pieces[src].at[pl.ds(start, n)], x.at[pl.ds(at, n)], sem.at[i]))
            at += n
        x_copies = list(first)
        waits = [[] for _ in range(blocks)]
        for i, (slot, src, start, n, to) in enumerate(code_map):
            target = w.at[slot // 2, pl.ds(to, n), pl.ds(slot % 2 * width, width)]
            waits[slot // 2].append(
                pltpu.make_async_copy(sources[src].at[pl.ds(start, n)], target, sem.at[len(row_map) + i])
            )
        down_copy = pltpu.make_async_copy(down, dn, sem.at[n_copies - 1])
        stages = [first + waits[0]] + waits[1:] + [[down_copy]]
        for stage in stages[:2]:
            for c in stage:
                c.start()
        for c in x_copies:
            c.wait()

        @pl.loop(0, blocks)
        def _(pair):
            for q in range(blocks):

                @pl.when(pair == q)
                def _(q=q):
                    for c in waits[q]:
                        c.wait()
                    if q + 2 < len(stages):
                        for c in stages[q + 2]:
                            c.start()

            @pl.loop(0, rows // tile)
            def _(part):
                at = pl.ds(pl.multiple_of(part * tile, tile), tile)
                acc = jnp.dot(x[at, :], w[pair], preferred_element_type=F32)
                for side in range(2):
                    slot = 2 * pair + side
                    proj[ids[slot], at] = acc[:, side * width : (side + 1) * width] * table[sidx[slot]]

        @pl.loop(0, rows // tile)
        def _(part):
            at = pl.ds(pl.multiple_of(part * tile, tile), tile)
            for b in range(blocks):
                gate, up = proj[b, at], proj[b + blocks, at]
                hid[at, b * width : (b + 1) * width] = (gate / (1.0 + jnp.exp(-gate)) * up).astype(BF16)

        down_copy.wait()

        def leave(n, slot):
            cols = pl.ds(pl.multiple_of(n * STEP, STEP), STEP)
            return [
                pltpu.make_async_copy(out.at[slot, pl.ds(at, n)], outs[i].at[:, cols], sem.at[base + slot * n_out + i])
                for i, (at, n) in enumerate(ranges)
            ]

        steps = depth // STEP

        @pl.loop(0, steps)
        def _(n):
            slot = lax.rem(n, 2)

            @pl.when(n >= 2)
            def _():
                for c in leave(n - 2, slot):
                    c.wait()

            cols = pl.ds(pl.multiple_of(n * STEP, STEP), STEP)

            @pl.loop(0, rows // tile)
            def _(part):
                at = pl.ds(pl.multiple_of(part * tile, tile), tile)
                out[slot, at] = jnp.dot(hid[at, :], dn[:, cols], preferred_element_type=F32).astype(BF16)

            for c in leave(n, slot):
                c.start()

        for n in (steps - 2, steps - 1):
            for c in leave(n, n % 2):
                c.wait()

    anywhere = pl.BlockSpec(memory_space=pltpu.HBM)
    smem = pl.BlockSpec(memory_space=pltpu.SMEM)
    return pl.pallas_call(
        kernel,
        out_shape=tuple(jax.ShapeDtypeStruct((n, depth), BF16) for _, n in ranges),
        in_specs=[smem] * 3 + [anywhere] * (n_codes + n_rows + 1),
        out_specs=(anywhere,) * n_out,
        scratch_shapes=[
            pltpu.VMEM((blocks, depth, 2 * width), BF16),
            pltpu.VMEM((rows, depth), BF16),
            pltpu.VMEM((local_ff, depth), BF16),
            pltpu.VMEM((slots, rows, width), F32),
            pltpu.VMEM((rows, local_ff), BF16),
            pltpu.VMEM((2, rows, STEP), BF16),
            pltpu.SemaphoreType.DMA((n_copies,)),
        ],
        compiler_params=pltpu.CompilerParams(vmem_limit_bytes=60 * 2**20),
        cost_estimate=pl.CostEstimate(
            flops=2 * rows * depth * local_ff * 3,
            bytes_accessed=2 * (depth * slots * width + local_ff * depth + 2 * rows * depth),
            transcendentals=rows * local_ff,
        ),
    )


def body(tokens, codes, block_ids, scale_idx, scale_table, down_weight):
    count, depth = tokens.shape
    width = codes.shape[2]
    local_ff = down_weight.shape[0]
    h_rows, h_depth = count // 2, depth // 2

    own = with_note(codes, block_ids, scale_idx)
    ca, cb = move(own, dy=1), move(own, dy=-1)
    ta, tb, tz = move(tokens, dx=1), move(tokens, dx=-1), move(tokens, zh=1)
    cz = move(after(own, tz), zl=1)
    y_top = move(rows_of(ca[:h_depth], ca[depth:]), dy=1)
    y_low = move(cb[h_depth:depth], dy=-1)
    taz, tbz = move(tz, dx=1), move(tz, dx=-1)
    cy = rows_of(y_top[:h_depth], y_low, y_top[h_depth:])
    top_in, low_in = rows_of(ta[:h_rows], taz[:h_rows]), rows_of(tb[h_rows:], tbz[h_rows:])
    cy = after(cy, cz)
    top_in, low_in = after((top_in, low_in), cy)
    caz, cbz, cyz = move(cz, dy=1), move(cz, dy=-1), move(cy, zl=1)
    x_top, x_low = move(top_in, dx=1), move(low_in, dx=-1)

    sources = [own, ca, cb, cz, cy, caz, cbz, cyz]
    code_map = [(i, i, 0, depth, 0) for i in range(8)]
    notes = jnp.stack([s[depth : depth + 2, 0] for s in sources]).astype(jnp.int32)
    ids, sidx = notes[:, 0], notes[:, 1]

    def swap(*pieces):
        return tuple(move(piece, core=1) for piece in pieces)

    def sums(ids, groups, cuts):
        pieces, row_map = [], []
        for piece, first, n in [g[0] for g in groups] + [g[1] for g in groups]:
            held = [i for i, p in enumerate(pieces) if p is piece]
            if not held:
                held = [len(pieces)]
                pieces.append(piece)
            row_map.append((held[0], first, n))
        ranges = [(sum(cuts[:i]), n) for i, n in enumerate(cuts)]
        run = feed_forward(code_map, row_map, ranges, depth, width, local_ff)
        return tuple(run(ids, sidx, scale_table, *sources, *pieces, down_weight))

    def whole(mine, sibling):
        return (mine, 0, count), (sibling, 0, count)

    def halves(p):
        return [
            ((mine, p * h_rows, h_rows), (sibling, p * h_rows, h_rows))
            for mine, sibling in ((x_top, o_top), (x_low, o_low))
        ]

    def add(*terms):
        total = terms[0].astype(F32)
        for term in terms[1:]:
            total = total + term.astype(F32)
        return total

    o_top, o_low, o_right_z, o_left_z = swap(x_top, x_low, tbz, taz)
    later = after((tb, ta, tz, tokens), o_top, o_low)
    o_right, o_left, o_z, o_own = swap(*later)
    part = sums(ids, halves(1) + [whole(tbz, o_right_z), whole(taz, o_left_z)], [count] * 6)
    part = after(part, o_right, o_left, o_z, o_own)
    got = swap(*part[3:])
    far_z, right, left = (add(part[i], got[i]).astype(BF16) for i in range(3))
    far_in, z_right, z_left = move(far_z, zh=1), move(right, dx=1), move(left, dx=-1)

    ids = after(ids, far_z, right, left)
    groups = halves(0) + [whole(tb, o_right), whole(ta, o_left), whole(tz, o_z)]
    part = sums(ids, groups, [count] * 4 + [h_rows] * 2 + [count] * 3)
    far, near, here_z, near_sib, here_sib = part[0], part[1:3], part[3], part[6:8], part[8]
    got = swap(*part[4:6])
    far, got, far_in, z_right, z_left = after((far, got, far_in, z_right, z_left))
    top = add(far[:h_rows], got[0], far_in[:h_rows]).astype(BF16)
    low = add(far[h_rows:], got[1], far_in[h_rows:]).astype(BF16)
    past_top, past_low = move(top, dx=1), move(low, dx=-1)

    near_sib, here_sib = after((near_sib, here_sib), top, low)
    got = swap(*near_sib, here_sib)
    ids = after(ids, top, low)
    here, own_sib = sums(ids, [whole(tokens, o_own)], [count] * 2)
    near, got, past_top, past_low, here = after((near, got, past_top, past_low, here))
    zero = jnp.zeros((), BF16)
    past_top = lax.pad(past_top, zero, ((0, h_rows, 0), (0, 0, 0)))
    past_low = lax.pad(past_low, zero, ((h_rows, 0, 0), (0, 0, 0)))
    right, left = (add(near[i], got[i], past).astype(BF16) for i, past in enumerate((past_top, past_low)))
    across = add(here_z, got[2], z_right, z_left).astype(BF16)
    right_in, left_in, across_in = move(right, dx=1), move(left, dx=-1), move(across, zh=1)
    own_sib = after(own_sib, right, left, across)
    return add(here, *swap(own_sib), right_in, left_in, across_in).astype(BF16)


def solution(mesh):
    return jax.shard_map(
        body,
        mesh=mesh,
        in_specs=(
            P(("dp", "tensor"), None),
            P(("dp", "tensor"), None, None),
            P(("dp", "tensor")),
            P(("dp", "tensor")),
            P(),
            P("tensor", None),
        ),
        out_specs=P(("dp", "tensor"), None),
        check_vma=False,
    )
```

```python
import jax
import jax.numpy as jnp
from jax import lax
from jax.experimental import pallas as pl
from jax.experimental.pallas import tpu as pltpu
from jax.sharding import PartitionSpec as P

NX, NY, NZL, NZH, NC = 4, 4, 2, 2, 2
AXES = ("dp", "tensor")
BF16, F32 = jnp.bfloat16, jnp.float32
NOTE = 16
STEP = 1024


def place(y, zl, zh, x, c):
    return ((y % NY * NZL + zl % NZL) * NZH + zh % NZH) * NX * NC + x % NX * NC + c % NC


def move(value, dx=0, dy=0, zl=0, zh=0, core=0):
    pairs = []
    for y in range(NY):
        for l in range(NZL):
            for h in range(NZH):
                for x in range(NX):
                    for c in range(NC):
                        pairs.append((place(y, l, h, x, c), place(y + dy, l + zl, h + zh, x + dx, c + core)))
    return lax.ppermute(value, AXES, pairs)


def after(value, *others):
    return lax.optimization_barrier((value,) + others)[0]


def rows_of(*parts):
    return jnp.concatenate(parts, axis=0)


def with_note(codes, block_ids, scale_idx):
    _, depth, width = codes.shape

    def kernel(number, entry, block, out, note, sem):
        big = pltpu.make_async_copy(block.at[0], out.at[pl.ds(0, depth)], sem.at[0])
        big.start()
        line = lax.broadcasted_iota(jnp.int32, (NOTE, width), 0)
        note[...] = jnp.where(line == 0, number[0], entry[0]).astype(F32).astype(BF16)
        small = pltpu.make_async_copy(note, out.at[pl.ds(depth, NOTE)], sem.at[1])
        small.start()
        small.wait()
        big.wait()

    smem = pl.BlockSpec(memory_space=pltpu.SMEM)
    anywhere = pl.BlockSpec(memory_space=pltpu.HBM)
    return pl.pallas_call(
        kernel,
        out_shape=jax.ShapeDtypeStruct((depth + NOTE, width), BF16),
        in_specs=[smem, smem, anywhere],
        out_specs=anywhere,
        scratch_shapes=[pltpu.VMEM((NOTE, width), BF16), pltpu.SemaphoreType.DMA((2,))],
        compiler_params=pltpu.CompilerParams(vmem_limit_bytes=2 * 2**20),
    )(block_ids, scale_idx, codes)


def join(pieces, plans):
    n_copies = sum(len(plan) for plan in plans)

    def kernel(*refs):
        sources, outs, sem = refs[: len(pieces)], refs[len(pieces) : -1], refs[-1]
        copies = []
        for plan, out in zip(plans, outs):
            at = 0
            for src, first, n in plan:
                copies.append(
                    pltpu.make_async_copy(sources[src].at[pl.ds(first, n)], out.at[pl.ds(at, n)], sem.at[len(copies)])
                )
                at += n
        for c in copies:
            c.start()
        for c in copies:
            c.wait()

    anywhere = pl.BlockSpec(memory_space=pl.ANY)
    return pl.pallas_call(
        kernel,
        out_shape=tuple(
            jax.ShapeDtypeStruct((sum(n for _, _, n in plan), pieces[plan[0][0]].shape[1]), BF16) for plan in plans
        ),
        in_specs=[anywhere] * len(pieces),
        out_specs=(anywhere,) * len(plans),
        scratch_shapes=[pltpu.SemaphoreType.DMA((n_copies,))],
        compiler_params=pltpu.CompilerParams(vmem_limit_bytes=2 * 2**20),
        cost_estimate=pl.CostEstimate(flops=1, bytes_accessed=1, transcendentals=0),
    )(*pieces)


def feed_forward(code_map, row_map, ranges, depth, width, local_ff, load):
    n_codes = 1 + max(m[1] for m in code_map) if load else 0
    n_rows = 1 + max(m[0] for m in row_map)
    slots = 1 + max(m[0] for m in code_map)
    blocks = slots // 2
    rows = sum(m[2] for m in row_map)
    tile = rows if rows <= 576 else rows // 2
    n_out = len(ranges)
    base = len(code_map) + len(row_map)
    n_copies = base + 1 + 2 * n_out

    def kernel(ids, sidx, table, *refs):
        sources, refs = refs[:n_codes], refs[n_codes:]
        pieces, refs = refs[:n_rows], refs[n_rows:]
        if load:
            down, outs, (w, dn, x, proj, hid, out, sem) = refs[0], refs[1 : 1 + n_out], refs[1 + n_out :]
        else:
            w, dn, outs, (x, proj, hid, out, sem) = refs[0], refs[1], refs[2 : 2 + n_out], refs[2 + n_out :]
        at = 0
        tiles = [[] for _ in range(rows // tile)]
        for i, (src, start, n) in enumerate(row_map):
            copy = pltpu.make_async_copy(pieces[src].at[pl.ds(start, n)], x.at[pl.ds(at, n)], sem.at[i])
            tiles[at // tile].append(copy)
            at += n
        x_copies = [c for copies in tiles for c in copies]
        if load:
            waits = [[] for _ in range(blocks)]
            for i, (slot, src, start, n, to) in enumerate(code_map):
                target = w.at[slot // 2, pl.ds(to, n), pl.ds(slot % 2 * width, width)]
                waits[slot // 2].append(
                    pltpu.make_async_copy(sources[src].at[pl.ds(start, n)], target, sem.at[len(row_map) + i])
                )
            down_copy = pltpu.make_async_copy(down, dn, sem.at[n_copies - 1])
            stages = [x_copies + waits[0]] + waits[1:] + [[down_copy]]
            for stage in stages[:2]:
                for c in stage:
                    c.start()
        else:
            for c in x_copies:
                c.start()
        for c in tiles[0]:
            c.wait()

        @pl.loop(0, blocks)
        def _(pair):
            if load:
                for q in range(blocks):

                    @pl.when(pair == q)
                    def _(q=q):
                        for c in waits[q]:
                            c.wait()
                        if q + 2 < len(stages):
                            for c in stages[q + 2]:
                                c.start()

            @pl.loop(0, rows // tile)
            def _(part):
                for t in range(1, rows // tile):

                    @pl.when((pair == 0) & (part == t))
                    def _(t=t):
                        for c in tiles[t]:
                            c.wait()

                at = pl.ds(pl.multiple_of(part * tile, tile), tile)
                acc = jnp.dot(x[at, :], w[pair], preferred_element_type=F32)
                for side in range(2):
                    slot = 2 * pair + side
                    proj[ids[slot], at] = acc[:, side * width : (side + 1) * width] * table[sidx[slot]]

        @pl.loop(0, rows // tile)
        def _(part):
            at = pl.ds(pl.multiple_of(part * tile, tile), tile)
            for b in range(blocks):
                gate, up = proj[b, at], proj[b + blocks, at]
                hid[at, b * width : (b + 1) * width] = (gate / (1.0 + jnp.exp(-gate)) * up).astype(BF16)

        if load:
            down_copy.wait()

        def leave(n, slot):
            cols = pl.ds(pl.multiple_of(n * STEP, STEP), STEP)
            return [
                pltpu.make_async_copy(out.at[slot, pl.ds(at, n)], outs[i].at[:, cols], sem.at[base + slot * n_out + i])
                for i, (at, n) in enumerate(ranges)
            ]

        steps = depth // STEP

        @pl.loop(0, steps)
        def _(n):
            slot = lax.rem(n, 2)

            @pl.when(n >= 2)
            def _():
                for c in leave(n - 2, slot):
                    c.wait()

            cols = pl.ds(pl.multiple_of(n * STEP, STEP), STEP)

            @pl.loop(0, rows // tile)
            def _(part):
                at = pl.ds(pl.multiple_of(part * tile, tile), tile)
                out[slot, at] = jnp.dot(hid[at, :], dn[:, cols], preferred_element_type=F32).astype(BF16)

            for c in leave(n, slot):
                c.start()

        for n in (steps - 2, steps - 1):
            for c in leave(n, n % 2):
                c.wait()

    anywhere = pl.BlockSpec(memory_space=pltpu.HBM)
    smem = pl.BlockSpec(memory_space=pltpu.SMEM)
    vmem = pl.BlockSpec(memory_space=pltpu.VMEM)
    results = tuple(jax.ShapeDtypeStruct((n, depth), BF16) for _, n in ranges)
    kept = (pltpu.VMEM((blocks, depth, 2 * width), BF16), pltpu.VMEM((local_ff, depth), BF16))
    return pl.pallas_call(
        kernel,
        out_shape=results + kept if load else results,
        in_specs=[smem] * 3 + [anywhere] * (n_codes + n_rows) + ([anywhere] if load else [vmem, vmem]),
        out_specs=(anywhere,) * n_out + ((vmem, vmem) if load else ()),
        scratch_shapes=[
            pltpu.VMEM((rows, depth), BF16),
            pltpu.VMEM((slots, rows, width), F32),
            pltpu.VMEM((rows, local_ff), BF16),
            pltpu.VMEM((2, rows, STEP), BF16),
            pltpu.SemaphoreType.DMA((n_copies,)),
        ],
        compiler_params=pltpu.CompilerParams(vmem_limit_bytes=44 * 2**20),
        cost_estimate=pl.CostEstimate(
            flops=2 * rows * depth * local_ff * 3,
            bytes_accessed=2 * (depth * slots * width + local_ff * depth + 2 * rows * depth),
            transcendentals=rows * local_ff,
        ),
    )


def body(tokens, codes, block_ids, scale_idx, scale_table, down_weight):
    count, depth = tokens.shape
    width = codes.shape[2]
    local_ff = down_weight.shape[0]
    h_rows, h_depth = count // 2, depth // 2

    own = with_note(codes, block_ids, scale_idx)
    ca, cb = move(own, dy=1), move(own, dy=-1)
    ta, tb, tz = move(tokens, dx=1), move(tokens, dx=-1), move(tokens, zh=1)
    cz = move(after(own, tz), zl=1)
    y_top = move(rows_of(ca[:h_depth], ca[depth:]), dy=1)
    y_low = move(cb[h_depth:depth], dy=-1)
    taz, tbz = move(tz, dx=1), move(tz, dx=-1)
    cy, top_in, low_in = join(
        (y_top, y_low, ta, taz, tb, tbz),
        (
            ((0, 0, h_depth), (1, 0, h_depth), (0, h_depth, NOTE)),
            ((2, 0, h_rows), (3, 0, h_rows)),
            ((4, h_rows, h_rows), (5, h_rows, h_rows)),
        ),
    )
    cy, top_in, low_in = after((cy, top_in, low_in), cz)
    caz, cbz, cyz = move(cz, dy=1), move(cz, dy=-1), move(cy, zl=1)
    x_top, x_low = move(top_in, dx=1), move(low_in, dx=-1)

    sources = [own, ca, cb, cz, cy, caz, cbz, cyz]
    code_map = [(i, i, 0, depth, 0) for i in range(8)]
    notes = jnp.stack([s[depth : depth + 2, 0] for s in sources]).astype(jnp.int32)
    ids, sidx = notes[:, 0], notes[:, 1]

    def swap(*pieces):
        return tuple(move(piece, core=1) for piece in pieces)

    def sums(ids, groups, cuts, weights=None):
        pieces, row_map = [], []
        for piece, first, n in [g[0] for g in groups] + [g[1] for g in groups]:
            held = [i for i, p in enumerate(pieces) if p is piece]
            if not held:
                held = [len(pieces)]
                pieces.append(piece)
            row_map.append((held[0], first, n))
        ranges = [(sum(cuts[:i]), n) for i, n in enumerate(cuts)]
        run = feed_forward(code_map, row_map, ranges, depth, width, local_ff, weights is None)
        if weights is None:
            return tuple(run(ids, sidx, scale_table, *sources, *pieces, down_weight))
        return tuple(run(ids, sidx, scale_table, *pieces, *weights))

    def whole(mine, sibling):
        return (mine, 0, count), (sibling, 0, count)

    def halves(p):
        return [
            ((mine, p * h_rows, h_rows), (sibling, p * h_rows, h_rows))
            for mine, sibling in ((x_top, o_top), (x_low, o_low))
        ]

    def add(*terms):
        total = terms[0].astype(F32)
        for term in terms[1:]:
            total = total + term.astype(F32)
        return total

    o_top, o_low, o_right_z, o_left_z = swap(x_top, x_low, tbz, taz)
    later = after((tb, ta, tz, tokens), o_top, o_low)
    o_right, o_left, o_z, o_own = swap(*later)
    part = sums(ids, halves(1) + [whole(tbz, o_right_z), whole(taz, o_left_z)], [count] * 6)
    part, weights = part[:6], part[6:]
    part = after(part, o_right, o_left, o_z, o_own)
    got = swap(*part[3:])
    far_z, right, left = (add(part[i], got[i]).astype(BF16) for i in range(3))
    far_in, z_right, z_left = move(far_z, zh=1), move(right, dx=1), move(left, dx=-1)

    ids = after(ids, far_z, right, left)
    groups = halves(0) + [whole(tb, o_right), whole(ta, o_left), whole(tz, o_z)]
    part = sums(ids, groups, [count] * 4 + [h_rows] * 2 + [count] * 3, weights)
    far, near, here_z, near_sib, here_sib = part[0], part[1:3], part[3], part[6:8], part[8]
    got = swap(*part[4:6])
    far, got, far_in, z_right, z_left = after((far, got, far_in, z_right, z_left))
    top = add(far[:h_rows], got[0], far_in[:h_rows]).astype(BF16)
    low = add(far[h_rows:], got[1], far_in[h_rows:]).astype(BF16)
    past_top, past_low = move(top, dx=1), move(low, dx=-1)

    near_sib, here_sib = after((near_sib, here_sib), top, low)
    got = swap(*near_sib, here_sib)
    ids = after(ids, top, low)
    here, own_sib = sums(ids, [whole(tokens, o_own)], [count] * 2, weights)
    near, got, past_top, past_low, here = after((near, got, past_top, past_low, here))
    zero = jnp.zeros((), BF16)
    past_top = lax.pad(past_top, zero, ((0, h_rows, 0), (0, 0, 0)))
    past_low = lax.pad(past_low, zero, ((h_rows, 0, 0), (0, 0, 0)))
    right, left = (add(near[i], got[i], past).astype(BF16) for i, past in enumerate((past_top, past_low)))
    across = add(here_z, got[2], z_right, z_left).astype(BF16)
    right_in, left_in, across_in = move(right, dx=1), move(left, dx=-1), move(across, zh=1)
    own_sib = after(own_sib, right, left, across)
    return add(here, *swap(own_sib), right_in, left_in, across_in).astype(BF16)


def solution(mesh):
    return jax.shard_map(
        body,
        mesh=mesh,
        in_specs=(
            P(("dp", "tensor"), None),
            P(("dp", "tensor"), None, None),
            P(("dp", "tensor")),
            P(("dp", "tensor")),
            P(),
            P("tensor", None),
        ),
        out_specs=P(("dp", "tensor"), None),
        check_vma=False,
    )
```

```python
import jax
import jax.numpy as jnp
from jax import lax
from jax.experimental import pallas as pl
from jax.experimental.pallas import tpu as pltpu
from jax.sharding import PartitionSpec as P

NX, NY, NZL, NZH, NC = 4, 4, 2, 2, 2
AXES = ("dp", "tensor")
BF16, F32 = jnp.bfloat16, jnp.float32
NOTE = 16
STEP = 1024


def place(y, zl, zh, x, c):
    return ((y % NY * NZL + zl % NZL) * NZH + zh % NZH) * NX * NC + x % NX * NC + c % NC


def move(value, dx=0, dy=0, zl=0, zh=0, core=0):
    pairs = []
    for y in range(NY):
        for l in range(NZL):
            for h in range(NZH):
                for x in range(NX):
                    for c in range(NC):
                        pairs.append((place(y, l, h, x, c), place(y + dy, l + zl, h + zh, x + dx, c + core)))
    return lax.ppermute(value, AXES, pairs)


def after(value, *others):
    return lax.optimization_barrier((value,) + others)[0]


def rows_of(*parts):
    return jnp.concatenate(parts, axis=0)


def with_note(codes, block_ids, scale_idx):
    _, depth, width = codes.shape

    def kernel(number, entry, block, out, note, sem):
        big = pltpu.make_async_copy(block.at[0], out.at[pl.ds(0, depth)], sem.at[0])
        big.start()
        line = lax.broadcasted_iota(jnp.int32, (NOTE, width), 0)
        note[...] = jnp.where(line == 0, number[0], entry[0]).astype(F32).astype(BF16)
        small = pltpu.make_async_copy(note, out.at[pl.ds(depth, NOTE)], sem.at[1])
        small.start()
        small.wait()
        big.wait()

    smem = pl.BlockSpec(memory_space=pltpu.SMEM)
    anywhere = pl.BlockSpec(memory_space=pltpu.HBM)
    return pl.pallas_call(
        kernel,
        out_shape=jax.ShapeDtypeStruct((depth + NOTE, width), BF16),
        in_specs=[smem, smem, anywhere],
        out_specs=anywhere,
        scratch_shapes=[pltpu.VMEM((NOTE, width), BF16), pltpu.SemaphoreType.DMA((2,))],
        compiler_params=pltpu.CompilerParams(vmem_limit_bytes=2 * 2**20),
    )(block_ids, scale_idx, codes)


def join(pieces, plans):
    n_copies = sum(len(plan) for plan in plans)

    def kernel(*refs):
        sources, outs, sem = refs[: len(pieces)], refs[len(pieces) : -1], refs[-1]
        copies = []
        for plan, out in zip(plans, outs):
            at = 0
            for src, first, n in plan:
                copies.append(
                    pltpu.make_async_copy(sources[src].at[pl.ds(first, n)], out.at[pl.ds(at, n)], sem.at[len(copies)])
                )
                at += n
        for c in copies:
            c.start()
        for c in copies:
            c.wait()

    anywhere = pl.BlockSpec(memory_space=pl.ANY)
    return pl.pallas_call(
        kernel,
        out_shape=tuple(
            jax.ShapeDtypeStruct((sum(n for _, _, n in plan), pieces[plan[0][0]].shape[1]), BF16) for plan in plans
        ),
        in_specs=[anywhere] * len(pieces),
        out_specs=(anywhere,) * len(plans),
        scratch_shapes=[pltpu.SemaphoreType.DMA((n_copies,))],
        compiler_params=pltpu.CompilerParams(vmem_limit_bytes=2 * 2**20),
        cost_estimate=pl.CostEstimate(flops=1, bytes_accessed=1, transcendentals=0),
    )(*pieces)


def feed_forward(code_map, row_map, ranges, depth, width, local_ff, load):
    n_codes = 1 + max(m[1] for m in code_map) if load else 0
    n_rows = 1 + max(m[0] for m in row_map)
    slots = 1 + max(m[0] for m in code_map)
    blocks = slots // 2
    rows = sum(m[2] for m in row_map)
    tile = rows if rows <= 576 else rows // 2
    n_out = len(ranges)
    base = len(code_map) + len(row_map)
    n_copies = base + 1 + 2 * n_out

    def kernel(ids, sidx, table, *refs):
        sources, refs = refs[:n_codes], refs[n_codes:]
        pieces, refs = refs[:n_rows], refs[n_rows:]
        if load:
            down, outs, (w, dn, x, proj, hid, out, sem) = refs[0], refs[1 : 1 + n_out], refs[1 + n_out :]
        else:
            w, dn, outs, (_, _, x, proj, hid, out, sem) = refs[0], refs[1], refs[2 : 2 + n_out], refs[2 + n_out :]
        at = 0
        tiles = [[] for _ in range(rows // tile)]
        for i, (src, start, n) in enumerate(row_map):
            copy = pltpu.make_async_copy(pieces[src].at[pl.ds(start, n)], x.at[pl.ds(at, n)], sem.at[i])
            tiles[at // tile].append(copy)
            at += n
        x_copies = [c for copies in tiles for c in copies]
        if load:
            waits = [[] for _ in range(blocks)]
            for i, (slot, src, start, n, to) in enumerate(code_map):
                target = w.at[slot // 2, pl.ds(to, n), pl.ds(slot % 2 * width, width)]
                waits[slot // 2].append(
                    pltpu.make_async_copy(sources[src].at[pl.ds(start, n)], target, sem.at[len(row_map) + i])
                )
            down_copy = pltpu.make_async_copy(down, dn, sem.at[n_copies - 1])
            stages = [x_copies + waits[0]] + waits[1:] + [[down_copy]]
            for stage in stages[:2]:
                for c in stage:
                    c.start()
        else:
            for c in x_copies:
                c.start()
        for c in tiles[0]:
            c.wait()

        @pl.loop(0, blocks)
        def _(pair):
            if load:
                for q in range(blocks):

                    @pl.when(pair == q)
                    def _(q=q):
                        for c in waits[q]:
                            c.wait()
                        if q + 2 < len(stages):
                            for c in stages[q + 2]:
                                c.start()

            @pl.loop(0, rows // tile)
            def _(part):
                for t in range(1, rows // tile):

                    @pl.when((pair == 0) & (part == t))
                    def _(t=t):
                        for c in tiles[t]:
                            c.wait()

                at = pl.ds(pl.multiple_of(part * tile, tile), tile)
                acc = jnp.dot(x[at, :], w[pair], preferred_element_type=F32)
                for side in range(2):
                    slot = 2 * pair + side
                    proj[ids[slot], at] = acc[:, side * width : (side + 1) * width] * table[sidx[slot]]

        @pl.loop(0, rows // tile)
        def _(part):
            at = pl.ds(pl.multiple_of(part * tile, tile), tile)
            for b in range(blocks):
                gate, up = proj[b, at], proj[b + blocks, at]
                hid[at, b * width : (b + 1) * width] = (gate / (1.0 + jnp.exp(-gate)) * up).astype(BF16)

        if load:
            down_copy.wait()

        def leave(n, slot):
            cols = pl.ds(pl.multiple_of(n * STEP, STEP), STEP)
            return [
                pltpu.make_async_copy(out.at[slot, pl.ds(at, n)], outs[i].at[:, cols], sem.at[base + slot * n_out + i])
                for i, (at, n) in enumerate(ranges)
            ]

        steps = depth // STEP

        @pl.loop(0, steps)
        def _(n):
            slot = lax.rem(n, 2)

            @pl.when(n >= 2)
            def _():
                for c in leave(n - 2, slot):
                    c.wait()

            cols = pl.ds(pl.multiple_of(n * STEP, STEP), STEP)

            @pl.loop(0, rows // tile)
            def _(part):
                at = pl.ds(pl.multiple_of(part * tile, tile), tile)
                out[slot, at] = jnp.dot(hid[at, :], dn[:, cols], preferred_element_type=F32).astype(BF16)

            for c in leave(n, slot):
                c.start()

        for n in (steps - 2, steps - 1):
            for c in leave(n, n % 2):
                c.wait()

    anywhere = pl.BlockSpec(memory_space=pltpu.HBM)
    smem = pl.BlockSpec(memory_space=pltpu.SMEM)
    vmem = pl.BlockSpec(memory_space=pltpu.VMEM)
    results = tuple(jax.ShapeDtypeStruct((n, depth), BF16) for _, n in ranges)
    kept = (pltpu.VMEM((blocks, depth, 2 * width), BF16), pltpu.VMEM((local_ff, depth), BF16))
    return pl.pallas_call(
        kernel,
        out_shape=results + kept,
        in_specs=[smem] * 3 + [anywhere] * (n_codes + n_rows) + ([anywhere] if load else [vmem, vmem]),
        out_specs=(anywhere,) * n_out + (vmem, vmem),
        input_output_aliases={} if load else {3 + n_rows: n_out, 4 + n_rows: n_out + 1},
        scratch_shapes=[
            pltpu.VMEM((rows, depth), BF16),
            pltpu.VMEM((slots, rows, width), F32),
            pltpu.VMEM((rows, local_ff), BF16),
            pltpu.VMEM((2, rows, STEP), BF16),
            pltpu.SemaphoreType.DMA((n_copies,)),
        ],
        compiler_params=pltpu.CompilerParams(vmem_limit_bytes=44 * 2**20),
        cost_estimate=pl.CostEstimate(
            flops=2 * rows * depth * local_ff * 3,
            bytes_accessed=2 * (depth * slots * width + local_ff * depth + 2 * rows * depth),
            transcendentals=rows * local_ff,
        ),
    )


def body(tokens, codes, block_ids, scale_idx, scale_table, down_weight):
    count, depth = tokens.shape
    width = codes.shape[2]
    local_ff = down_weight.shape[0]
    h_rows, h_depth = count // 2, depth // 2

    own = with_note(codes, block_ids, scale_idx)
    ca, cb = move(own, dy=1), move(own, dy=-1)
    ta, tb, tz = move(tokens, dx=1), move(tokens, dx=-1), move(tokens, zh=1)
    cz = move(after(own, tz), zl=1)
    y_top = move(rows_of(ca[:h_depth], ca[depth:]), dy=1)
    y_low = move(cb[h_depth:depth], dy=-1)
    taz, tbz = move(tz, dx=1), move(tz, dx=-1)
    cy, top_in, low_in = join(
        (y_top, y_low, ta, taz, tb, tbz),
        (
            ((0, 0, h_depth), (1, 0, h_depth), (0, h_depth, NOTE)),
            ((2, 0, h_rows), (3, 0, h_rows)),
            ((4, h_rows, h_rows), (5, h_rows, h_rows)),
        ),
    )
    cy, top_in, low_in = after((cy, top_in, low_in), cz)
    caz, cbz, cyz = move(cz, dy=1), move(cz, dy=-1), move(cy, zl=1)
    x_top, x_low = move(top_in, dx=1), move(low_in, dx=-1)

    sources = [own, ca, cb, cz, cy, caz, cbz, cyz]
    code_map = [(i, i, 0, depth, 0) for i in range(8)]
    notes = jnp.stack([s[depth : depth + 2, 0] for s in sources]).astype(jnp.int32)
    ids, sidx = notes[:, 0], notes[:, 1]

    def swap(*pieces):
        return tuple(move(piece, core=1) for piece in pieces)

    def sums(ids, groups, cuts, weights=None):
        pieces, row_map = [], []
        for piece, first, n in [g[0] for g in groups] + [g[1] for g in groups]:
            held = [i for i, p in enumerate(pieces) if p is piece]
            if not held:
                held = [len(pieces)]
                pieces.append(piece)
            row_map.append((held[0], first, n))
        ranges = [(sum(cuts[:i]), n) for i, n in enumerate(cuts)]
        run = feed_forward(code_map, row_map, ranges, depth, width, local_ff, weights is None)
        if weights is None:
            return tuple(run(ids, sidx, scale_table, *sources, *pieces, down_weight))
        return tuple(run(ids, sidx, scale_table, *pieces, *weights))

    def whole(mine, sibling):
        return (mine, 0, count), (sibling, 0, count)

    def halves(p):
        return [
            ((mine, p * h_rows, h_rows), (sibling, p * h_rows, h_rows))
            for mine, sibling in ((x_top, o_top), (x_low, o_low))
        ]

    def add(*terms):
        total = terms[0].astype(F32)
        for term in terms[1:]:
            total = total + term.astype(F32)
        return total

    o_top, o_low, o_right_z, o_left_z = swap(x_top, x_low, tbz, taz)
    later = after((tb, ta, tz, tokens), o_top, o_low)
    o_right, o_left, o_z, o_own = swap(*later)
    part = sums(ids, halves(1) + [whole(tbz, o_right_z), whole(taz, o_left_z)], [count] * 6)
    part, weights = part[:6], part[6:]
    part = after(part, o_right, o_left, o_z, o_own)
    got = swap(*part[3:])
    far_z, right, left = (add(part[i], got[i]).astype(BF16) for i in range(3))
    far_in, z_right, z_left = move(far_z, zh=1), move(right, dx=1), move(left, dx=-1)

    ids = after(ids, far_z, right, left)
    groups = halves(0) + [whole(tb, o_right), whole(ta, o_left), whole(tz, o_z)]
    part = sums(ids, groups, [count] * 4 + [h_rows] * 2 + [count] * 3, weights)
    part, weights = part[:9], part[9:]
    far, near, here_z, near_sib, here_sib = part[0], part[1:3], part[3], part[6:8], part[8]
    got = swap(*part[4:6])
    far, got, far_in, z_right, z_left = after((far, got, far_in, z_right, z_left))
    top = add(far[:h_rows], got[0], far_in[:h_rows]).astype(BF16)
    low = add(far[h_rows:], got[1], far_in[h_rows:]).astype(BF16)
    past_top, past_low = move(top, dx=1), move(low, dx=-1)

    near_sib, here_sib = after((near_sib, here_sib), top, low)
    got = swap(*near_sib, here_sib)
    ids = after(ids, top, low)
    here, own_sib = sums(ids, [whole(tokens, o_own)], [count] * 2, weights)[:2]
    near, got, past_top, past_low, here = after((near, got, past_top, past_low, here))
    zero = jnp.zeros((), BF16)
    past_top = lax.pad(past_top, zero, ((0, h_rows, 0), (0, 0, 0)))
    past_low = lax.pad(past_low, zero, ((h_rows, 0, 0), (0, 0, 0)))
    right, left = (add(near[i], got[i], past).astype(BF16) for i, past in enumerate((past_top, past_low)))
    across = add(here_z, got[2], z_right, z_left).astype(BF16)
    right_in, left_in, across_in = move(right, dx=1), move(left, dx=-1), move(across, zh=1)
    own_sib = after(own_sib, right, left, across)
    return add(here, *swap(own_sib), right_in, left_in, across_in).astype(BF16)


def solution(mesh):
    return jax.shard_map(
        body,
        mesh=mesh,
        in_specs=(
            P(("dp", "tensor"), None),
            P(("dp", "tensor"), None, None),
            P(("dp", "tensor")),
            P(("dp", "tensor")),
            P(),
            P("tensor", None),
        ),
        out_specs=P(("dp", "tensor"), None),
        check_vma=False,
    )
```

```python
import jax
import jax.numpy as jnp
from jax import lax
from jax.experimental import pallas as pl
from jax.experimental.pallas import tpu as pltpu
from jax.sharding import PartitionSpec as P

NX, NY, NZL, NZH, NC = 4, 4, 2, 2, 2
AXES = ("dp", "tensor")
BF16, F32 = jnp.bfloat16, jnp.float32
NOTE = 16
STEP = 1024


def place(y, zl, zh, x, c):
    return ((y % NY * NZL + zl % NZL) * NZH + zh % NZH) * NX * NC + x % NX * NC + c % NC


def move(value, dx=0, dy=0, zl=0, zh=0, core=0):
    pairs = []
    for y in range(NY):
        for l in range(NZL):
            for h in range(NZH):
                for x in range(NX):
                    for c in range(NC):
                        pairs.append((place(y, l, h, x, c), place(y + dy, l + zl, h + zh, x + dx, c + core)))
    return lax.ppermute(value, AXES, pairs)


def after(value, *others):
    return lax.optimization_barrier((value,) + others)[0]


def rows_of(*parts):
    return jnp.concatenate(parts, axis=0)


def with_note(codes, block_ids, scale_idx):
    _, depth, width = codes.shape

    def kernel(number, entry, block, out, note, sem):
        big = pltpu.make_async_copy(block.at[0], out.at[pl.ds(0, depth)], sem.at[0])
        big.start()
        line = lax.broadcasted_iota(jnp.int32, (NOTE, width), 0)
        note[...] = jnp.where(line == 0, number[0], entry[0]).astype(F32).astype(BF16)
        small = pltpu.make_async_copy(note, out.at[pl.ds(depth, NOTE)], sem.at[1])
        small.start()
        small.wait()
        big.wait()

    smem = pl.BlockSpec(memory_space=pltpu.SMEM)
    anywhere = pl.BlockSpec(memory_space=pltpu.HBM)
    return pl.pallas_call(
        kernel,
        out_shape=jax.ShapeDtypeStruct((depth + NOTE, width), BF16),
        in_specs=[smem, smem, anywhere],
        out_specs=anywhere,
        scratch_shapes=[pltpu.VMEM((NOTE, width), BF16), pltpu.SemaphoreType.DMA((2,))],
        compiler_params=pltpu.CompilerParams(vmem_limit_bytes=2 * 2**20),
    )(block_ids, scale_idx, codes)


def join(pieces, plans):
    n_copies = sum(len(plan) for plan in plans)

    def kernel(*refs):
        sources, outs, sem = refs[: len(pieces)], refs[len(pieces) : -1], refs[-1]
        copies = []
        for plan, out in zip(plans, outs):
            at = 0
            for src, first, n in plan:
                copies.append(
                    pltpu.make_async_copy(sources[src].at[pl.ds(first, n)], out.at[pl.ds(at, n)], sem.at[len(copies)])
                )
                at += n
        for c in copies:
            c.start()
        for c in copies:
            c.wait()

    anywhere = pl.BlockSpec(memory_space=pl.ANY)
    return pl.pallas_call(
        kernel,
        out_shape=tuple(
            jax.ShapeDtypeStruct((sum(n for _, _, n in plan), pieces[plan[0][0]].shape[1]), BF16) for plan in plans
        ),
        in_specs=[anywhere] * len(pieces),
        out_specs=(anywhere,) * len(plans),
        scratch_shapes=[pltpu.SemaphoreType.DMA((n_copies,))],
        compiler_params=pltpu.CompilerParams(vmem_limit_bytes=2 * 2**20),
        cost_estimate=pl.CostEstimate(flops=1, bytes_accessed=1, transcendentals=0),
    )(*pieces)


def feed_forward(code_map, row_map, ranges, depth, width, local_ff, load):
    n_codes = 1 + max(m[1] for m in code_map) if load else 0
    n_rows = 1 + max(m[0] for m in row_map)
    slots = 1 + max(m[0] for m in code_map)
    blocks = slots // 2
    rows = sum(m[2] for m in row_map)
    tile = rows if rows <= 576 else rows // 2
    n_out = len(ranges)
    base = len(code_map) + len(row_map)
    n_copies = base + 1 + 2 * n_out

    def kernel(ids, sidx, table, *refs):
        sources, refs = refs[:n_codes], refs[n_codes:]
        pieces, refs = refs[:n_rows], refs[n_rows:]
        if load:
            down, outs, (w, dn, x, proj, hid, out, sem) = refs[0], refs[1 : 1 + n_out], refs[1 + n_out :]
        else:
            w, dn, outs, (_, _, x, proj, hid, out, sem) = refs[0], refs[1], refs[2 : 2 + n_out], refs[2 + n_out :]
        at = 0
        tiles = [[] for _ in range(rows // tile)]
        for i, (src, start, n) in enumerate(row_map):
            copy = pltpu.make_async_copy(pieces[src].at[pl.ds(start, n)], x.at[pl.ds(at, n)], sem.at[i])
            tiles[at // tile].append(copy)
            at += n
        x_copies = [c for copies in tiles for c in copies]
        if load:
            waits = [[] for _ in range(blocks)]
            for i, (slot, src, start, n, to) in enumerate(code_map):
                target = w.at[slot // 2, pl.ds(to, n), pl.ds(slot % 2 * width, width)]
                waits[slot // 2].append(
                    pltpu.make_async_copy(sources[src].at[pl.ds(start, n)], target, sem.at[len(row_map) + i])
                )
            down_copy = pltpu.make_async_copy(down, dn, sem.at[n_copies - 1])
            stages = [x_copies + waits[0]] + waits[1:] + [[down_copy]]
            for stage in stages[:2]:
                for c in stage:
                    c.start()
        else:
            for c in x_copies:
                c.start()
        for c in tiles[0]:
            c.wait()

        @pl.loop(0, blocks)
        def _(pair):
            if load:
                for q in range(blocks):

                    @pl.when(pair == q)
                    def _(q=q):
                        for c in waits[q]:
                            c.wait()
                        if q + 2 < len(stages):
                            for c in stages[q + 2]:
                                c.start()

            @pl.loop(0, rows // tile)
            def _(part):
                for t in range(1, rows // tile):

                    @pl.when((pair == 0) & (part == t))
                    def _(t=t):
                        for c in tiles[t]:
                            c.wait()

                at = pl.ds(pl.multiple_of(part * tile, tile), tile)
                acc = jnp.dot(x[at, :], w[pair], preferred_element_type=F32)
                for side in range(2):
                    slot = 2 * pair + side
                    proj[ids[slot], at] = acc[:, side * width : (side + 1) * width] * table[sidx[slot]]

        @pl.loop(0, rows // tile)
        def _(part):
            at = pl.ds(pl.multiple_of(part * tile, tile), tile)
            for b in range(blocks):
                gate, up = proj[b, at], proj[b + blocks, at]
                hid[at, b * width : (b + 1) * width] = (gate / (1.0 + jnp.exp(-gate)) * up).astype(BF16)

        if load:
            down_copy.wait()

        def leave(n, slot):
            cols = pl.ds(pl.multiple_of(n * STEP, STEP), STEP)
            return [
                pltpu.make_async_copy(out.at[slot, pl.ds(at, n)], outs[i].at[:, cols], sem.at[base + slot * n_out + i])
                for i, (at, n) in enumerate(ranges)
            ]

        steps = depth // STEP

        @pl.loop(0, steps)
        def _(n):
            slot = lax.rem(n, 2)

            @pl.when(n >= 2)
            def _():
                for c in leave(n - 2, slot):
                    c.wait()

            cols = pl.ds(pl.multiple_of(n * STEP, STEP), STEP)

            @pl.loop(0, rows // tile)
            def _(part):
                at = pl.ds(pl.multiple_of(part * tile, tile), tile)
                out[slot, at] = jnp.dot(hid[at, :], dn[:, cols], preferred_element_type=F32).astype(BF16)

            for c in leave(n, slot):
                c.start()

        for n in (steps - 2, steps - 1):
            for c in leave(n, n % 2):
                c.wait()

    anywhere = pl.BlockSpec(memory_space=pltpu.HBM)
    smem = pl.BlockSpec(memory_space=pltpu.SMEM)
    vmem = pl.BlockSpec(memory_space=pltpu.VMEM)
    results = tuple(jax.ShapeDtypeStruct((n, depth), BF16) for _, n in ranges)
    kept = (pltpu.VMEM((blocks, depth, 2 * width), BF16), pltpu.VMEM((local_ff, depth), BF16))
    return pl.pallas_call(
        kernel,
        out_shape=results + kept,
        in_specs=[smem] * 3 + [anywhere] * (n_codes + n_rows) + ([anywhere] if load else [vmem, vmem]),
        out_specs=(anywhere,) * n_out + (vmem, vmem),
        input_output_aliases={} if load else {3 + n_rows: n_out, 4 + n_rows: n_out + 1},
        scratch_shapes=[
            pltpu.VMEM((rows, depth), BF16),
            pltpu.VMEM((slots, rows, width), F32),
            pltpu.VMEM((rows, local_ff), BF16),
            pltpu.VMEM((2, rows, STEP), BF16),
            pltpu.SemaphoreType.DMA((n_copies,)),
        ],
        compiler_params=pltpu.CompilerParams(vmem_limit_bytes=44 * 2**20),
        cost_estimate=pl.CostEstimate(
            flops=2 * rows * depth * local_ff * 3,
            bytes_accessed=2 * (depth * slots * width + local_ff * depth + 2 * rows * depth),
            transcendentals=rows * local_ff,
        ),
    )


def body(tokens, codes, block_ids, scale_idx, scale_table, down_weight):
    count, depth = tokens.shape
    width = codes.shape[2]
    local_ff = down_weight.shape[0]
    h_rows, h_depth = count // 2, depth // 2

    own = with_note(codes, block_ids, scale_idx)
    ca, cb = move(own, dy=1), move(own, dy=-1)
    ta, tb, tz = move(tokens, dx=1), move(tokens, dx=-1), move(tokens, zh=1)
    cz = move(after(own, tz), zl=1)
    y_top = move(rows_of(ca[:h_depth], ca[depth:]), dy=1)
    y_low = move(cb[h_depth:depth], dy=-1)
    tz_x = after(tz, ta, tb)
    taz, tbz = move(tz_x, dx=1), move(tz_x, dx=-1)
    cy, top_in, low_in = join(
        (y_top, y_low, ta, taz, tb, tbz),
        (
            ((0, 0, h_depth), (1, 0, h_depth), (0, h_depth, NOTE)),
            ((2, 0, h_rows), (3, 0, h_rows)),
            ((4, h_rows, h_rows), (5, h_rows, h_rows)),
        ),
    )
    cy, cz_y = after((cy, cz), top_in)
    caz, cbz, cyz = move(cz_y, dy=1), move(cz_y, dy=-1), move(cy, zl=1)
    x_top, x_low = move(top_in, dx=1), move(low_in, dx=-1)

    sources = [own, ca, cb, cz, cy, caz, cbz, cyz]
    code_map = [(i, i, 0, depth, 0) for i in range(8)]
    notes = jnp.stack([s[depth : depth + 2, 0] for s in sources]).astype(jnp.int32)
    ids, sidx = notes[:, 0], notes[:, 1]

    def swap(*pieces):
        return tuple(move(piece, core=1) for piece in pieces)

    def sums(ids, groups, cuts, weights=None):
        pieces, row_map = [], []
        for piece, first, n in [g[0] for g in groups] + [g[1] for g in groups]:
            held = [i for i, p in enumerate(pieces) if p is piece]
            if not held:
                held = [len(pieces)]
                pieces.append(piece)
            row_map.append((held[0], first, n))
        ranges = [(sum(cuts[:i]), n) for i, n in enumerate(cuts)]
        run = feed_forward(code_map, row_map, ranges, depth, width, local_ff, weights is None)
        if weights is None:
            return tuple(run(ids, sidx, scale_table, *sources, *pieces, down_weight))
        return tuple(run(ids, sidx, scale_table, *pieces, *weights))

    def whole(mine, sibling):
        return (mine, 0, count), (sibling, 0, count)

    def halves(p):
        return [
            ((mine, p * h_rows, h_rows), (sibling, p * h_rows, h_rows))
            for mine, sibling in ((x_top, o_top), (x_low, o_low))
        ]

    def add(*terms):
        total = terms[0].astype(F32)
        for term in terms[1:]:
            total = total + term.astype(F32)
        return total

    o_top, o_low, o_right_z, o_left_z = swap(x_top, x_low, tbz, taz)
    later = after((tb, ta, tz, tokens), o_top, o_low)
    o_right, o_left, o_z, o_own = swap(*later)
    part = sums(ids, halves(1) + [whole(tbz, o_right_z), whole(taz, o_left_z)], [count] * 6)
    part, weights = part[:6], part[6:]
    part = after(part, o_right, o_left, o_z, o_own)
    got = swap(*part[3:])
    far_z, right, left = (add(part[i], got[i]).astype(BF16) for i in range(3))
    far_in, z_right, z_left = move(far_z, zh=1), move(right, dx=1), move(left, dx=-1)

    ids = after(ids, far_z, right, left)
    groups = halves(0) + [whole(tb, o_right), whole(ta, o_left), whole(tz, o_z)]
    part = sums(ids, groups, [count] * 4 + [h_rows] * 2 + [count] * 3, weights)
    part, weights = part[:9], part[9:]
    far, near, here_z, near_sib, here_sib = part[0], part[1:3], part[3], part[6:8], part[8]
    got = swap(*part[4:6])
    far, got, far_in, z_right, z_left = after((far, got, far_in, z_right, z_left))
    top = add(far[:h_rows], got[0], far_in[:h_rows]).astype(BF16)
    low = add(far[h_rows:], got[1], far_in[h_rows:]).astype(BF16)
    past_top, past_low = move(top, dx=1), move(low, dx=-1)

    near_sib, here_sib = after((near_sib, here_sib), top, low)
    got = swap(*near_sib, here_sib)
    ids = after(ids, top, low)
    here, own_sib = sums(ids, [whole(tokens, o_own)], [count] * 2, weights)[:2]
    near, got, past_top, past_low, here = after((near, got, past_top, past_low, here))
    zero = jnp.zeros((), BF16)
    past_top = lax.pad(past_top, zero, ((0, h_rows, 0), (0, 0, 0)))
    past_low = lax.pad(past_low, zero, ((h_rows, 0, 0), (0, 0, 0)))
    right, left = (add(near[i], got[i], past).astype(BF16) for i, past in enumerate((past_top, past_low)))
    across = add(here_z, got[2], z_right, z_left).astype(BF16)
    right_in, left_in, across_in = move(right, dx=1), move(left, dx=-1), move(across, zh=1)
    own_sib = after(own_sib, right, left, across)
    return add(here, *swap(own_sib), right_in, left_in, across_in).astype(BF16)


def solution(mesh):
    return jax.shard_map(
        body,
        mesh=mesh,
        in_specs=(
            P(("dp", "tensor"), None),
            P(("dp", "tensor"), None, None),
            P(("dp", "tensor")),
            P(("dp", "tensor")),
            P(),
            P("tensor", None),
        ),
        out_specs=P(("dp", "tensor"), None),
        check_vma=False,
    )
```

```python
import jax
import jax.numpy as jnp
from jax import lax
from jax.experimental import pallas as pl
from jax.experimental.pallas import tpu as pltpu
from jax.sharding import PartitionSpec as P

NX, NY, NZL, NZH, NC = 4, 4, 2, 2, 2
AXES = ("dp", "tensor")
BF16, F32 = jnp.bfloat16, jnp.float32
NOTE = 16
STEP = 1024


def place(y, zl, zh, x, c):
    return ((y % NY * NZL + zl % NZL) * NZH + zh % NZH) * NX * NC + x % NX * NC + c % NC


def move(value, dx=0, dy=0, zl=0, zh=0, core=0):
    pairs = []
    for y in range(NY):
        for l in range(NZL):
            for h in range(NZH):
                for x in range(NX):
                    for c in range(NC):
                        pairs.append((place(y, l, h, x, c), place(y + dy, l + zl, h + zh, x + dx, c + core)))
    return lax.ppermute(value, AXES, pairs)


def after(value, *others):
    return lax.optimization_barrier((value,) + others)[0]


def rows_of(*parts):
    return jnp.concatenate(parts, axis=0)


def with_note(codes, block_ids, scale_idx):
    _, depth, width = codes.shape

    def kernel(number, entry, block, out, note, sem):
        big = pltpu.make_async_copy(block.at[0], out.at[pl.ds(0, depth)], sem.at[0])
        big.start()
        line = lax.broadcasted_iota(jnp.int32, (NOTE, width), 0)
        note[...] = jnp.where(line == 0, number[0], entry[0]).astype(F32).astype(BF16)
        small = pltpu.make_async_copy(note, out.at[pl.ds(depth, NOTE)], sem.at[1])
        small.start()
        small.wait()
        big.wait()

    smem = pl.BlockSpec(memory_space=pltpu.SMEM)
    anywhere = pl.BlockSpec(memory_space=pltpu.HBM)
    return pl.pallas_call(
        kernel,
        out_shape=jax.ShapeDtypeStruct((depth + NOTE, width), BF16),
        in_specs=[smem, smem, anywhere],
        out_specs=anywhere,
        scratch_shapes=[pltpu.VMEM((NOTE, width), BF16), pltpu.SemaphoreType.DMA((2,))],
        compiler_params=pltpu.CompilerParams(vmem_limit_bytes=2 * 2**20),
    )(block_ids, scale_idx, codes)


def join(pieces, plans):
    n_copies = sum(len(plan) for plan in plans)

    def kernel(*refs):
        sources, outs, sem = refs[: len(pieces)], refs[len(pieces) : -1], refs[-1]
        copies = []
        for plan, out in zip(plans, outs):
            at = 0
            for src, first, n in plan:
                copies.append(
                    pltpu.make_async_copy(sources[src].at[pl.ds(first, n)], out.at[pl.ds(at, n)], sem.at[len(copies)])
                )
                at += n
        for c in copies:
            c.start()
        for c in copies:
            c.wait()

    anywhere = pl.BlockSpec(memory_space=pl.ANY)
    return pl.pallas_call(
        kernel,
        out_shape=tuple(
            jax.ShapeDtypeStruct((sum(n for _, _, n in plan), pieces[plan[0][0]].shape[1]), BF16) for plan in plans
        ),
        in_specs=[anywhere] * len(pieces),
        out_specs=(anywhere,) * len(plans),
        scratch_shapes=[pltpu.SemaphoreType.DMA((n_copies,))],
        compiler_params=pltpu.CompilerParams(vmem_limit_bytes=2 * 2**20),
        cost_estimate=pl.CostEstimate(flops=1, bytes_accessed=1, transcendentals=0),
    )(*pieces)


def feed_forward(code_map, row_map, ranges, depth, width, local_ff, load):
    n_codes = 1 + max(m[1] for m in code_map) if load else 0
    n_rows = 1 + max(m[0] for m in row_map)
    slots = 1 + max(m[0] for m in code_map)
    blocks = slots // 2
    rows = sum(m[2] for m in row_map)
    tile = rows if rows <= 576 else rows // 2
    n_out = len(ranges)
    base = len(code_map) + len(row_map)
    n_copies = base + 1 + 2 * n_out

    def kernel(ids, sidx, table, *refs):
        sources, refs = refs[:n_codes], refs[n_codes:]
        pieces, refs = refs[:n_rows], refs[n_rows:]
        if load:
            down, outs, (w, dn, x, proj, hid, out, sem) = refs[0], refs[1 : 1 + n_out], refs[1 + n_out :]
        else:
            w, dn, outs, (_, _, x, proj, hid, out, sem) = refs[0], refs[1], refs[2 : 2 + n_out], refs[2 + n_out :]
        at = 0
        tiles = [[] for _ in range(rows // tile)]
        for i, (src, start, n) in enumerate(row_map):
            copy = pltpu.make_async_copy(pieces[src].at[pl.ds(start, n)], x.at[pl.ds(at, n)], sem.at[i])
            tiles[at // tile].append(copy)
            at += n
        x_copies = [c for copies in tiles for c in copies]
        if load:
            waits = [[] for _ in range(blocks)]
            for i, (slot, src, start, n, to) in enumerate(code_map):
                target = w.at[slot // 2, pl.ds(to, n), pl.ds(slot % 2 * width, width)]
                waits[slot // 2].append(
                    pltpu.make_async_copy(sources[src].at[pl.ds(start, n)], target, sem.at[len(row_map) + i])
                )
            down_copy = pltpu.make_async_copy(down, dn, sem.at[n_copies - 1])
            stages = [x_copies + waits[0]] + waits[1:] + [[down_copy]]
            for stage in stages[:2]:
                for c in stage:
                    c.start()
        else:
            for c in x_copies:
                c.start()
        for c in tiles[0]:
            c.wait()

        @pl.loop(0, blocks)
        def _(pair):
            if load:
                for q in range(blocks):

                    @pl.when(pair == q)
                    def _(q=q):
                        for c in waits[q]:
                            c.wait()
                        if q + 2 < len(stages):
                            for c in stages[q + 2]:
                                c.start()

            @pl.loop(0, rows // tile)
            def _(part):
                for t in range(1, rows // tile):

                    @pl.when((pair == 0) & (part == t))
                    def _(t=t):
                        for c in tiles[t]:
                            c.wait()

                at = pl.ds(pl.multiple_of(part * tile, tile), tile)
                acc = jnp.dot(x[at, :], w[pair], preferred_element_type=F32)
                for side in range(2):
                    slot = 2 * pair + side
                    proj[ids[slot], at] = acc[:, side * width : (side + 1) * width] * table[sidx[slot]]

        @pl.loop(0, rows // tile)
        def _(part):
            at = pl.ds(pl.multiple_of(part * tile, tile), tile)
            for b in range(blocks):
                gate, up = proj[b, at], proj[b + blocks, at]
                hid[at, b * width : (b + 1) * width] = (gate / (1.0 + jnp.exp(-gate)) * up).astype(BF16)

        if load:
            down_copy.wait()

        def leave(n, slot):
            cols = pl.ds(pl.multiple_of(n * STEP, STEP), STEP)
            return [
                pltpu.make_async_copy(out.at[slot, pl.ds(at, n)], outs[i].at[:, cols], sem.at[base + slot * n_out + i])
                for i, (at, n) in enumerate(ranges)
            ]

        steps = depth // STEP

        @pl.loop(0, steps)
        def _(n):
            slot = lax.rem(n, 2)

            @pl.when(n >= 2)
            def _():
                for c in leave(n - 2, slot):
                    c.wait()

            cols = pl.ds(pl.multiple_of(n * STEP, STEP), STEP)

            @pl.loop(0, rows // tile)
            def _(part):
                at = pl.ds(pl.multiple_of(part * tile, tile), tile)
                out[slot, at] = jnp.dot(hid[at, :], dn[:, cols], preferred_element_type=F32).astype(BF16)

            for c in leave(n, slot):
                c.start()

        for n in (steps - 2, steps - 1):
            for c in leave(n, n % 2):
                c.wait()

    anywhere = pl.BlockSpec(memory_space=pltpu.HBM)
    smem = pl.BlockSpec(memory_space=pltpu.SMEM)
    vmem = pl.BlockSpec(memory_space=pltpu.VMEM)
    results = tuple(jax.ShapeDtypeStruct((n, depth), BF16) for _, n in ranges)
    kept = (pltpu.VMEM((blocks, depth, 2 * width), BF16), pltpu.VMEM((local_ff, depth), BF16))
    return pl.pallas_call(
        kernel,
        out_shape=results + kept,
        in_specs=[smem] * 3 + [anywhere] * (n_codes + n_rows) + ([anywhere] if load else [vmem, vmem]),
        out_specs=(anywhere,) * n_out + (vmem, vmem),
        input_output_aliases={} if load else {3 + n_rows: n_out, 4 + n_rows: n_out + 1},
        scratch_shapes=[
            pltpu.VMEM((rows, depth), BF16),
            pltpu.VMEM((slots, rows, width), F32),
            pltpu.VMEM((rows, local_ff), BF16),
            pltpu.VMEM((2, rows, STEP), BF16),
            pltpu.SemaphoreType.DMA((n_copies,)),
        ],
        compiler_params=pltpu.CompilerParams(vmem_limit_bytes=44 * 2**20),
        cost_estimate=pl.CostEstimate(
            flops=2 * rows * depth * local_ff * 3,
            bytes_accessed=2 * (depth * slots * width + local_ff * depth + 2 * rows * depth),
            transcendentals=rows * local_ff,
        ),
    )


def body(tokens, codes, block_ids, scale_idx, scale_table, down_weight):
    count, depth = tokens.shape
    width = codes.shape[2]
    local_ff = down_weight.shape[0]
    h_rows, h_depth = count // 2, depth // 2

    own = with_note(codes, block_ids, scale_idx)
    ca, cb = move(own, dy=1), move(own, dy=-1)
    ta, tb, tz = move(tokens, dx=1), move(tokens, dx=-1), move(tokens, zh=1)
    cz = move(after(own, tz), zl=1)
    y_top = move(rows_of(ca[:h_depth], ca[depth:]), dy=1)
    y_low = move(cb[h_depth:depth], dy=-1)
    tz_x = after(tz, ta, tb)
    taz, tbz = move(tz_x, dx=1), move(tz_x, dx=-1)
    cy, top_in, low_in = join(
        (y_top, y_low, ta, taz, tb, tbz),
        (
            ((0, 0, h_depth), (1, 0, h_depth), (0, h_depth, NOTE)),
            ((2, 0, h_rows), (3, 0, h_rows)),
            ((4, h_rows, h_rows), (5, h_rows, h_rows)),
        ),
    )
    cy, cz_y = after((cy, cz), top_in)
    caz, cbz, cyz = move(cz_y, dy=1), move(cz_y, dy=-1), move(cy, zl=1)
    x_top, x_low = move(top_in, dx=1), move(low_in, dx=-1)

    sources = [own, ca, cb, cz, cy, caz, cbz, cyz]
    code_map = [(i, i, 0, depth, 0) for i in range(8)]
    notes = jnp.stack([s[depth : depth + 2, 0] for s in sources]).astype(jnp.int32)
    ids, sidx = notes[:, 0], notes[:, 1]

    def swap(*pieces):
        return tuple(move(piece, core=1) for piece in pieces)

    def sums(ids, groups, cuts, weights=None):
        pieces, row_map = [], []
        for piece, first, n in [g[0] for g in groups] + [g[1] for g in groups]:
            held = [i for i, p in enumerate(pieces) if p is piece]
            if not held:
                held = [len(pieces)]
                pieces.append(piece)
            row_map.append((held[0], first, n))
        ranges = [(sum(cuts[:i]), n) for i, n in enumerate(cuts)]
        run = feed_forward(code_map, row_map, ranges, depth, width, local_ff, weights is None)
        if weights is None:
            return tuple(run(ids, sidx, scale_table, *sources, *pieces, down_weight))
        return tuple(run(ids, sidx, scale_table, *pieces, *weights))

    def whole(mine, sibling):
        return (mine, 0, count), (sibling, 0, count)

    def halves(p):
        return [
            ((mine, p * h_rows, h_rows), (sibling, p * h_rows, h_rows))
            for mine, sibling in ((x_top, o_top), (x_low, o_low))
        ]

    def add(*terms):
        total = terms[0].astype(F32)
        for term in terms[1:]:
            total = total + term.astype(F32)
        return total

    o_top, o_low, o_right_z, o_left_z = swap(x_top, x_low, tbz, taz)
    later = after((tb, ta, tz, tokens), o_top, o_low)
    o_right, o_left, o_z, o_own = swap(*later)
    part = sums(ids, halves(1) + [whole(tbz, o_right_z), whole(taz, o_left_z)], [count] * 6)
    part, weights = part[:6], part[6:]
    part = after(part, o_right, o_left, o_z, o_own)
    got = swap(*part[3:])
    far_z, right, left = (add(part[i], got[i]).astype(BF16) for i in range(3))
    far_in, z_right, z_left = move(far_z, zh=1), move(right, dx=1), move(left, dx=-1)

    ids = after(ids, far_z, right, left)
    groups = halves(0) + [whole(tb, o_right), whole(ta, o_left), whole(tz, o_z)]
    part = sums(ids, groups, [count] + [h_rows] * 4 + [count] + [h_rows] * 6 + [count], weights)
    part, weights = part[:13], part[13:]
    got = swap(*part[6:8])
    part, got, far_in, z_right, z_left = after((part, got, far_in, z_right, z_left))
    far, near, here_z, near_sib, z_sib = part[0], part[1:5], part[5], part[8:12], part[12]
    top = add(far[:h_rows], got[0], far_in[:h_rows]).astype(BF16)
    low = add(far[h_rows:], got[1], far_in[h_rows:]).astype(BF16)
    past_top, past_low = move(top, dx=1), move(low, dx=-1)
    got = swap(near_sib[1], near_sib[2], z_sib)
    right, left = add(near[1], got[0]).astype(BF16), add(near[2], got[1]).astype(BF16)
    across = add(here_z, got[2], z_right, z_left).astype(BF16)
    right_bottom, left_top, across_in = move(right, dx=1), move(left, dx=-1), move(across, zh=1)

    ids = after(ids, top, low, right, left, across)
    here, own_sib = sums(ids, [whole(tokens, o_own)], [count] * 2, weights)[:2]
    held = after((here, near, near_sib, past_top, past_low, right_bottom, left_top, across_in))
    here, near, near_sib, past_top, past_low, right_bottom, left_top, across_in = held
    got = swap(near_sib[0], near_sib[3])
    right, left = add(near[0], got[0], past_top).astype(BF16), add(near[3], got[1], past_low).astype(BF16)
    right_top, left_bottom = move(right, dx=1), move(left, dx=-1)
    own_sib = after(own_sib, right, left)
    total = add(here, *swap(own_sib), across_in)
    zero = jnp.zeros((), BF16)
    for first, piece in ((0, right_top), (h_rows, right_bottom), (0, left_top), (h_rows, left_bottom)):
        total = total + lax.pad(piece, zero, ((first, h_rows - first, 0), (0, 0, 0))).astype(F32)
    return total.astype(BF16)


def solution(mesh):
    return jax.shard_map(
        body,
        mesh=mesh,
        in_specs=(
            P(("dp", "tensor"), None),
            P(("dp", "tensor"), None, None),
            P(("dp", "tensor")),
            P(("dp", "tensor")),
            P(),
            P("tensor", None),
        ),
        out_specs=P(("dp", "tensor"), None),
        check_vma=False,
    )
```

```python
import jax
import jax.numpy as jnp
from jax import lax
from jax.experimental import pallas as pl
from jax.experimental.pallas import tpu as pltpu
from jax.sharding import PartitionSpec as P

NX, NY, NZL, NZH, NC = 4, 4, 2, 2, 2
AXES = ("dp", "tensor")
BF16, F32 = jnp.bfloat16, jnp.float32
NOTE = 16
STEP = 1024


def place(y, zl, zh, x, c):
    return ((y % NY * NZL + zl % NZL) * NZH + zh % NZH) * NX * NC + x % NX * NC + c % NC


def move(value, dx=0, dy=0, zl=0, zh=0, core=0):
    pairs = []
    for y in range(NY):
        for l in range(NZL):
            for h in range(NZH):
                for x in range(NX):
                    for c in range(NC):
                        pairs.append((place(y, l, h, x, c), place(y + dy, l + zl, h + zh, x + dx, c + core)))
    return lax.ppermute(value, AXES, pairs)


def after(value, *others):
    return lax.optimization_barrier((value,) + others)[0]


def rows_of(*parts):
    return jnp.concatenate(parts, axis=0)


def with_note(codes, block_ids, scale_idx):
    _, depth, width = codes.shape

    def kernel(number, entry, block, out, note, sem):
        big = pltpu.make_async_copy(block.at[0], out.at[pl.ds(0, depth)], sem.at[0])
        big.start()
        line = lax.broadcasted_iota(jnp.int32, (NOTE, width), 0)
        note[...] = jnp.where(line == 0, number[0], entry[0]).astype(F32).astype(BF16)
        small = pltpu.make_async_copy(note, out.at[pl.ds(depth, NOTE)], sem.at[1])
        small.start()
        small.wait()
        big.wait()

    smem = pl.BlockSpec(memory_space=pltpu.SMEM)
    anywhere = pl.BlockSpec(memory_space=pltpu.HBM)
    return pl.pallas_call(
        kernel,
        out_shape=jax.ShapeDtypeStruct((depth + NOTE, width), BF16),
        in_specs=[smem, smem, anywhere],
        out_specs=anywhere,
        scratch_shapes=[pltpu.VMEM((NOTE, width), BF16), pltpu.SemaphoreType.DMA((2,))],
        compiler_params=pltpu.CompilerParams(vmem_limit_bytes=2 * 2**20),
    )(block_ids, scale_idx, codes)


def join(pieces, plans):
    n_copies = sum(len(plan) for plan in plans)

    def kernel(*refs):
        sources, outs, sem = refs[: len(pieces)], refs[len(pieces) : -1], refs[-1]
        copies = []
        for plan, out in zip(plans, outs):
            at = 0
            for src, first, n in plan:
                copies.append(
                    pltpu.make_async_copy(sources[src].at[pl.ds(first, n)], out.at[pl.ds(at, n)], sem.at[len(copies)])
                )
                at += n
        for c in copies:
            c.start()
        for c in copies:
            c.wait()

    anywhere = pl.BlockSpec(memory_space=pl.ANY)
    return pl.pallas_call(
        kernel,
        out_shape=tuple(
            jax.ShapeDtypeStruct((sum(n for _, _, n in plan), pieces[plan[0][0]].shape[1]), BF16) for plan in plans
        ),
        in_specs=[anywhere] * len(pieces),
        out_specs=(anywhere,) * len(plans),
        scratch_shapes=[pltpu.SemaphoreType.DMA((n_copies,))],
        compiler_params=pltpu.CompilerParams(vmem_limit_bytes=2 * 2**20),
        cost_estimate=pl.CostEstimate(flops=1, bytes_accessed=1, transcendentals=0),
    )(*pieces)


def feed_forward(code_map, row_map, ranges, depth, width, local_ff, load):
    n_codes = 1 + max(m[1] for m in code_map) if load else 0
    n_rows = 1 + max(m[0] for m in row_map)
    slots = 1 + max(m[0] for m in code_map)
    blocks = slots // 2
    rows = sum(m[2] for m in row_map)
    tile = rows if rows <= 576 else rows // 2
    n_out = len(ranges)
    base = len(code_map) + len(row_map)
    n_copies = base + 1 + 2 * n_out

    def kernel(ids, sidx, table, *refs):
        sources, refs = refs[:n_codes], refs[n_codes:]
        pieces, refs = refs[:n_rows], refs[n_rows:]
        if load:
            down, outs, (w, dn, x, proj, hid, out, sem) = refs[0], refs[1 : 1 + n_out], refs[1 + n_out :]
        else:
            w, dn, outs, (_, _, x, proj, hid, out, sem) = refs[0], refs[1], refs[2 : 2 + n_out], refs[2 + n_out :]
        at = 0
        tiles = [[] for _ in range(rows // tile)]
        for i, (src, start, n) in enumerate(row_map):
            copy = pltpu.make_async_copy(pieces[src].at[pl.ds(start, n)], x.at[pl.ds(at, n)], sem.at[i])
            tiles[at // tile].append(copy)
            at += n
        x_copies = [c for copies in tiles for c in copies]
        if load:
            waits = [[] for _ in range(blocks)]
            for i, (slot, src, start, n, to) in enumerate(code_map):
                target = w.at[slot // 2, pl.ds(to, n), pl.ds(slot % 2 * width, width)]
                waits[slot // 2].append(
                    pltpu.make_async_copy(sources[src].at[pl.ds(start, n)], target, sem.at[len(row_map) + i])
                )
            down_copy = pltpu.make_async_copy(down, dn, sem.at[n_copies - 1])
            stages = [x_copies + waits[0]] + waits[1:] + [[down_copy]]
            for stage in stages[:2]:
                for c in stage:
                    c.start()
        else:
            for c in x_copies:
                c.start()
        for c in tiles[0]:
            c.wait()

        @pl.loop(0, blocks)
        def _(pair):
            if load:
                for q in range(blocks):

                    @pl.when(pair == q)
                    def _(q=q):
                        for c in waits[q]:
                            c.wait()
                        if q + 2 < len(stages):
                            for c in stages[q + 2]:
                                c.start()

            @pl.loop(0, rows // tile)
            def _(part):
                for t in range(1, rows // tile):

                    @pl.when((pair == 0) & (part == t))
                    def _(t=t):
                        for c in tiles[t]:
                            c.wait()

                at = pl.ds(pl.multiple_of(part * tile, tile), tile)
                acc = jnp.dot(x[at, :], w[pair], preferred_element_type=F32)
                for side in range(2):
                    slot = 2 * pair + side
                    proj[ids[slot], at] = acc[:, side * width : (side + 1) * width] * table[sidx[slot]]

        @pl.loop(0, rows // tile)
        def _(part):
            at = pl.ds(pl.multiple_of(part * tile, tile), tile)
            for b in range(blocks):
                gate, up = proj[b, at], proj[b + blocks, at]
                hid[at, b * width : (b + 1) * width] = (gate / (1.0 + jnp.exp(-gate)) * up).astype(BF16)

        if load:
            down_copy.wait()

        def leave(n, slot):
            cols = pl.ds(pl.multiple_of(n * STEP, STEP), STEP)
            return [
                pltpu.make_async_copy(out.at[slot, pl.ds(at, n)], outs[i].at[:, cols], sem.at[base + slot * n_out + i])
                for i, (at, n) in enumerate(ranges)
            ]

        steps = depth // STEP

        @pl.loop(0, steps)
        def _(n):
            slot = lax.rem(n, 2)

            @pl.when(n >= 2)
            def _():
                for c in leave(n - 2, slot):
                    c.wait()

            cols = pl.ds(pl.multiple_of(n * STEP, STEP), STEP)

            @pl.loop(0, rows // tile)
            def _(part):
                at = pl.ds(pl.multiple_of(part * tile, tile), tile)
                out[slot, at] = jnp.dot(hid[at, :], dn[:, cols], preferred_element_type=F32).astype(BF16)

            for c in leave(n, slot):
                c.start()

        for n in (steps - 2, steps - 1):
            for c in leave(n, n % 2):
                c.wait()

    anywhere = pl.BlockSpec(memory_space=pltpu.HBM)
    smem = pl.BlockSpec(memory_space=pltpu.SMEM)
    vmem = pl.BlockSpec(memory_space=pltpu.VMEM)
    results = tuple(jax.ShapeDtypeStruct((n, depth), BF16) for _, n in ranges)
    kept = (pltpu.VMEM((blocks, depth, 2 * width), BF16), pltpu.VMEM((local_ff, depth), BF16))
    return pl.pallas_call(
        kernel,
        out_shape=results + kept,
        in_specs=[smem] * 3 + [anywhere] * (n_codes + n_rows) + ([anywhere] if load else [vmem, vmem]),
        out_specs=(anywhere,) * n_out + (vmem, vmem),
        input_output_aliases={} if load else {3 + n_rows: n_out, 4 + n_rows: n_out + 1},
        scratch_shapes=[
            pltpu.VMEM((rows, depth), BF16),
            pltpu.VMEM((slots, rows, width), F32),
            pltpu.VMEM((rows, local_ff), BF16),
            pltpu.VMEM((2, rows, STEP), BF16),
            pltpu.SemaphoreType.DMA((n_copies,)),
        ],
        compiler_params=pltpu.CompilerParams(vmem_limit_bytes=44 * 2**20),
        cost_estimate=pl.CostEstimate(
            flops=2 * rows * depth * local_ff * 3,
            bytes_accessed=2 * (depth * slots * width + local_ff * depth + 2 * rows * depth),
            transcendentals=rows * local_ff,
        ),
    )


def body(tokens, codes, block_ids, scale_idx, scale_table, down_weight):
    count, depth = tokens.shape
    width = codes.shape[2]
    local_ff = down_weight.shape[0]
    h_rows, h_depth = count // 2, depth // 2

    own = with_note(codes, block_ids, scale_idx)
    ca, cb = move(own, dy=1), move(own, dy=-1)
    ta, tb, tz = move(tokens, dx=1), move(tokens, dx=-1), move(tokens, zh=1)
    cz = move(after(own, tz), zl=1)
    y_top = move(rows_of(ca[:h_depth], ca[depth:]), dy=1)
    y_low = move(cb[h_depth:depth], dy=-1)
    tz_x = after(tz, ta, tb)
    taz, tbz = move(tz_x, dx=1), move(tz_x, dx=-1)
    cy, top_in, low_in = join(
        (y_top, y_low, ta, taz, tb, tbz),
        (
            ((0, 0, h_depth), (1, 0, h_depth), (0, h_depth, NOTE)),
            ((2, 0, h_rows), (3, 0, h_rows)),
            ((4, h_rows, h_rows), (5, h_rows, h_rows)),
        ),
    )
    cy, cz_y = after((cy, cz), top_in)
    caz, cbz, cyz = move(cz_y, dy=1), move(cz_y, dy=-1), move(cy, zl=1)
    x_top, x_low = move(top_in, dx=1), move(low_in, dx=-1)

    sources = [own, ca, cb, cz, cy, caz, cbz, cyz]
    code_map = [(i, i, 0, depth, 0) for i in range(8)]
    notes = jnp.stack([s[depth : depth + 2, 0] for s in sources]).astype(jnp.int32)
    ids, sidx = notes[:, 0], notes[:, 1]

    def swap(*pieces):
        return tuple(move(piece, core=1) for piece in pieces)

    def sums(ids, groups, cuts, weights=None):
        pieces, row_map = [], []
        for piece, first, n in [g[0] for g in groups] + [g[1] for g in groups]:
            held = [i for i, p in enumerate(pieces) if p is piece]
            if not held:
                held = [len(pieces)]
                pieces.append(piece)
            row_map.append((held[0], first, n))
        ranges = [(sum(cuts[:i]), n) for i, n in enumerate(cuts)]
        run = feed_forward(code_map, row_map, ranges, depth, width, local_ff, weights is None)
        if weights is None:
            return tuple(run(ids, sidx, scale_table, *sources, *pieces, down_weight))
        return tuple(run(ids, sidx, scale_table, *pieces, *weights))

    def whole(mine, sibling):
        return (mine, 0, count), (sibling, 0, count)

    def halves(p):
        return [
            ((mine, p * h_rows, h_rows), (sibling, p * h_rows, h_rows))
            for mine, sibling in ((x_top, o_top), (x_low, o_low))
        ]

    def add(*terms):
        total = terms[0].astype(F32)
        for term in terms[1:]:
            total = total + term.astype(F32)
        return total

    o_top, o_low, o_right_z, o_left_z = swap(x_top, x_low, tbz, taz)
    later = after((tb, ta, tz, tokens), o_top, o_low)
    o_right, o_left, o_z, o_own = swap(*later)
    part = sums(ids, halves(1) + [whole(tbz, o_right_z), whole(taz, o_left_z)], [count] * 6)
    part, weights = part[:6], part[6:]
    part = after(part, o_right, o_left, o_z, o_own)
    got = swap(*part[3:])
    right, left = (add(part[i], got[i]).astype(BF16) for i in (1, 2))
    far_z = add(after(part[0], right, left), got[0]).astype(BF16)
    far_in, z_right, z_left = move(far_z, zh=1), move(right, dx=1), move(left, dx=-1)

    ids = after(ids, far_z, right, left)
    groups = halves(0) + [whole(tb, o_right), whole(ta, o_left)]
    part = sums(ids, groups, [count] * 3 + [h_rows] * 2 + [count] * 2, weights)
    part, weights = part[:7], part[7:]
    far, near, near_sib = part[0], part[1:3], part[5:7]
    got = swap(*part[3:5])
    far, got, z_right, z_left, far_in = after((far, got, z_right, z_left, far_in))
    top = add(far[:h_rows], got[0], far_in[:h_rows]).astype(BF16)
    low = add(far[h_rows:], got[1], far_in[h_rows:]).astype(BF16)
    past_top, past_low = move(top, dx=1), move(low, dx=-1)

    near_sib = after(near_sib, top, low)
    got = swap(*near_sib)
    ids = after(ids, top, low)
    here_z, here, z_sib, own_sib = sums(ids, [whole(tz, o_z), whole(tokens, o_own)], [count] * 4, weights)[:4]
    near, got, past_top, past_low, here_z = after((near, got, past_top, past_low, here_z))
    zero = jnp.zeros((), BF16)
    past_top = lax.pad(past_top, zero, ((0, h_rows, 0), (0, 0, 0)))
    past_low = lax.pad(past_low, zero, ((h_rows, 0, 0), (0, 0, 0)))
    right, left = (add(near[i], got[i], past).astype(BF16) for i, past in enumerate((past_top, past_low)))
    z_sib, own_sib = after((z_sib, own_sib), near, past_top, past_low)
    across = add(here_z, *swap(z_sib), z_right, z_left).astype(BF16)
    right_in, left_in, across_in = move(right, dx=1), move(left, dx=-1), move(across, zh=1)
    own_sib = after(own_sib, right, left, across)
    return add(here, *swap(own_sib), right_in, left_in, across_in).astype(BF16)


def solution(mesh):
    return jax.shard_map(
        body,
        mesh=mesh,
        in_specs=(
            P(("dp", "tensor"), None),
            P(("dp", "tensor"), None, None),
            P(("dp", "tensor")),
            P(("dp", "tensor")),
            P(),
            P("tensor", None),
        ),
        out_specs=P(("dp", "tensor"), None),
        check_vma=False,
    )
```

```python
import jax
import jax.numpy as jnp
from jax import lax
from jax.experimental import pallas as pl
from jax.experimental.pallas import tpu as pltpu
from jax.sharding import PartitionSpec as P

NX, NY, NZL, NZH, NC = 4, 4, 2, 2, 2
AXES = ("dp", "tensor")
BF16, F32 = jnp.bfloat16, jnp.float32
NOTE = 16
STEP = 1024


def place(y, zl, zh, x, c):
    return ((y % NY * NZL + zl % NZL) * NZH + zh % NZH) * NX * NC + x % NX * NC + c % NC


def move(value, dx=0, dy=0, zl=0, zh=0, core=0):
    pairs = []
    for y in range(NY):
        for l in range(NZL):
            for h in range(NZH):
                for x in range(NX):
                    for c in range(NC):
                        pairs.append((place(y, l, h, x, c), place(y + dy, l + zl, h + zh, x + dx, c + core)))
    return lax.ppermute(value, AXES, pairs)


def after(value, *others):
    return lax.optimization_barrier((value,) + others)[0]


def rows_of(*parts):
    return jnp.concatenate(parts, axis=0)


def with_note(codes, block_ids, scale_idx):
    _, depth, width = codes.shape

    def kernel(number, entry, block, out, note, sem):
        big = pltpu.make_async_copy(block.at[0], out.at[pl.ds(0, depth)], sem.at[0])
        big.start()
        line = lax.broadcasted_iota(jnp.int32, (NOTE, width), 0)
        note[...] = jnp.where(line == 0, number[0], entry[0]).astype(F32).astype(BF16)
        small = pltpu.make_async_copy(note, out.at[pl.ds(depth, NOTE)], sem.at[1])
        small.start()
        small.wait()
        big.wait()

    smem = pl.BlockSpec(memory_space=pltpu.SMEM)
    anywhere = pl.BlockSpec(memory_space=pltpu.HBM)
    return pl.pallas_call(
        kernel,
        out_shape=jax.ShapeDtypeStruct((depth + NOTE, width), BF16),
        in_specs=[smem, smem, anywhere],
        out_specs=anywhere,
        scratch_shapes=[pltpu.VMEM((NOTE, width), BF16), pltpu.SemaphoreType.DMA((2,))],
        compiler_params=pltpu.CompilerParams(vmem_limit_bytes=2 * 2**20),
    )(block_ids, scale_idx, codes)


def join(pieces, plans):
    n_copies = sum(len(plan) for plan in plans)

    def kernel(*refs):
        sources, outs, sem = refs[: len(pieces)], refs[len(pieces) : -1], refs[-1]
        copies = []
        for plan, out in zip(plans, outs):
            at = 0
            for src, first, n in plan:
                copies.append(
                    pltpu.make_async_copy(sources[src].at[pl.ds(first, n)], out.at[pl.ds(at, n)], sem.at[len(copies)])
                )
                at += n
        for c in copies:
            c.start()
        for c in copies:
            c.wait()

    anywhere = pl.BlockSpec(memory_space=pl.ANY)
    return pl.pallas_call(
        kernel,
        out_shape=tuple(
            jax.ShapeDtypeStruct((sum(n for _, _, n in plan), pieces[plan[0][0]].shape[1]), BF16) for plan in plans
        ),
        in_specs=[anywhere] * len(pieces),
        out_specs=(anywhere,) * len(plans),
        scratch_shapes=[pltpu.SemaphoreType.DMA((n_copies,))],
        compiler_params=pltpu.CompilerParams(vmem_limit_bytes=2 * 2**20),
        cost_estimate=pl.CostEstimate(flops=1, bytes_accessed=1, transcendentals=0),
    )(*pieces)


def feed_forward(code_map, row_map, ranges, depth, width, local_ff, load):
    n_codes = 1 + max(m[1] for m in code_map) if load else 0
    n_rows = 1 + max(m[0] for m in row_map)
    slots = 1 + max(m[0] for m in code_map)
    blocks = slots // 2
    rows = sum(m[2] for m in row_map)
    tile = rows if rows <= 576 else rows // 2
    n_out = len(ranges)
    base = len(code_map) + len(row_map)
    n_copies = base + 1 + 2 * n_out

    def kernel(ids, sidx, table, *refs):
        sources, refs = refs[:n_codes], refs[n_codes:]
        pieces, refs = refs[:n_rows], refs[n_rows:]
        if load:
            down, outs, (w, dn, x, proj, hid, out, sem) = refs[0], refs[1 : 1 + n_out], refs[1 + n_out :]
        else:
            w, dn, outs, (_, _, x, proj, hid, out, sem) = refs[0], refs[1], refs[2 : 2 + n_out], refs[2 + n_out :]
        at = 0
        tiles = [[] for _ in range(rows // tile)]
        for i, (src, start, n) in enumerate(row_map):
            copy = pltpu.make_async_copy(pieces[src].at[pl.ds(start, n)], x.at[pl.ds(at, n)], sem.at[i])
            tiles[at // tile].append(copy)
            at += n
        x_copies = [c for copies in tiles for c in copies]
        if load:
            waits = [[] for _ in range(blocks)]
            for i, (slot, src, start, n, to) in enumerate(code_map):
                target = w.at[slot // 2, pl.ds(to, n), pl.ds(slot % 2 * width, width)]
                waits[slot // 2].append(
                    pltpu.make_async_copy(sources[src].at[pl.ds(start, n)], target, sem.at[len(row_map) + i])
                )
            down_copy = pltpu.make_async_copy(down, dn, sem.at[n_copies - 1])
            stages = [x_copies + waits[0]] + waits[1:] + [[down_copy]]
            for stage in stages[:2]:
                for c in stage:
                    c.start()
        else:
            for c in x_copies:
                c.start()
        for c in tiles[0]:
            c.wait()

        @pl.loop(0, blocks)
        def _(pair):
            if load:
                for q in range(blocks):

                    @pl.when(pair == q)
                    def _(q=q):
                        for c in waits[q]:
                            c.wait()
                        if q + 2 < len(stages):
                            for c in stages[q + 2]:
                                c.start()

            @pl.loop(0, rows // tile)
            def _(part):
                for t in range(1, rows // tile):

                    @pl.when((pair == 0) & (part == t))
                    def _(t=t):
                        for c in tiles[t]:
                            c.wait()

                at = pl.ds(pl.multiple_of(part * tile, tile), tile)
                acc = jnp.dot(x[at, :], w[pair], preferred_element_type=F32)
                for side in range(2):
                    slot = 2 * pair + side
                    proj[ids[slot], at] = acc[:, side * width : (side + 1) * width] * table[sidx[slot]]

        @pl.loop(0, rows // tile)
        def _(part):
            at = pl.ds(pl.multiple_of(part * tile, tile), tile)
            for b in range(blocks):
                gate, up = proj[b, at], proj[b + blocks, at]
                hid[at, b * width : (b + 1) * width] = (gate / (1.0 + jnp.exp(-gate)) * up).astype(BF16)

        if load:
            down_copy.wait()

        def leave(n, slot):
            cols = pl.ds(pl.multiple_of(n * STEP, STEP), STEP)
            return [
                pltpu.make_async_copy(out.at[slot, pl.ds(at, n)], outs[i].at[:, cols], sem.at[base + slot * n_out + i])
                for i, (at, n) in enumerate(ranges)
            ]

        steps = depth // STEP

        @pl.loop(0, steps)
        def _(n):
            slot = lax.rem(n, 2)

            @pl.when(n >= 2)
            def _():
                for c in leave(n - 2, slot):
                    c.wait()

            cols = pl.ds(pl.multiple_of(n * STEP, STEP), STEP)

            @pl.loop(0, rows // tile)
            def _(part):
                at = pl.ds(pl.multiple_of(part * tile, tile), tile)
                out[slot, at] = jnp.dot(hid[at, :], dn[:, cols], preferred_element_type=F32).astype(BF16)

            for c in leave(n, slot):
                c.start()

        for n in (steps - 2, steps - 1):
            for c in leave(n, n % 2):
                c.wait()

    anywhere = pl.BlockSpec(memory_space=pltpu.HBM)
    smem = pl.BlockSpec(memory_space=pltpu.SMEM)
    vmem = pl.BlockSpec(memory_space=pltpu.VMEM)
    results = tuple(jax.ShapeDtypeStruct((n, depth), BF16) for _, n in ranges)
    kept = (pltpu.VMEM((blocks, depth, 2 * width), BF16), pltpu.VMEM((local_ff, depth), BF16))
    return pl.pallas_call(
        kernel,
        out_shape=results + kept,
        in_specs=[smem] * 3 + [anywhere] * (n_codes + n_rows) + ([anywhere] if load else [vmem, vmem]),
        out_specs=(anywhere,) * n_out + (vmem, vmem),
        input_output_aliases={} if load else {3 + n_rows: n_out, 4 + n_rows: n_out + 1},
        scratch_shapes=[
            pltpu.VMEM((rows, depth), BF16),
            pltpu.VMEM((slots, rows, width), F32),
            pltpu.VMEM((rows, local_ff), BF16),
            pltpu.VMEM((2, rows, STEP), BF16),
            pltpu.SemaphoreType.DMA((n_copies,)),
        ],
        compiler_params=pltpu.CompilerParams(vmem_limit_bytes=44 * 2**20),
        cost_estimate=pl.CostEstimate(
            flops=2 * rows * depth * local_ff * 3,
            bytes_accessed=2 * (depth * slots * width + local_ff * depth + 2 * rows * depth),
            transcendentals=rows * local_ff,
        ),
    )


def body(tokens, codes, block_ids, scale_idx, scale_table, down_weight):
    count, depth = tokens.shape
    width = codes.shape[2]
    local_ff = down_weight.shape[0]
    h_rows, h_depth = count // 2, depth // 2

    own = with_note(codes, block_ids, scale_idx)
    ca, cb = move(own, dy=1), move(own, dy=-1)
    ta, tb, tz = move(tokens, dx=1), move(tokens, dx=-1), move(tokens, zh=1)
    cz = move(after(own, tz), zl=1)
    y_top = move(rows_of(ca[:h_depth], ca[depth:]), dy=1)
    y_low = move(cb[h_depth:depth], dy=-1)
    tz_x = after(tz, ta, tb)
    taz, tbz = move(tz_x, dx=1), move(tz_x, dx=-1)
    cy, top_in, low_in = join(
        (y_top, y_low, ta, taz, tb, tbz),
        (
            ((0, 0, h_depth), (1, 0, h_depth), (0, h_depth, NOTE)),
            ((2, 0, h_rows), (3, 0, h_rows)),
            ((4, h_rows, h_rows), (5, h_rows, h_rows)),
        ),
    )
    cy, cz_y = after((cy, cz), top_in)
    caz, cbz, cyz = move(cz_y, dy=1), move(cz_y, dy=-1), move(cy, zl=1)
    x_top, x_low = move(top_in, dx=1), move(low_in, dx=-1)

    sources = [own, ca, cb, cz, cy, caz, cbz, cyz]
    code_map = [(i, i, 0, depth, 0) for i in range(8)]
    notes = jnp.stack([s[depth : depth + 2, 0] for s in sources]).astype(jnp.int32)
    ids, sidx = notes[:, 0], notes[:, 1]

    def swap(*pieces):
        return tuple(move(piece, core=1) for piece in pieces)

    def sums(ids, groups, cuts, weights=None):
        pieces, row_map = [], []
        for piece, first, n in [g[0] for g in groups] + [g[1] for g in groups]:
            held = [i for i, p in enumerate(pieces) if p is piece]
            if not held:
                held = [len(pieces)]
                pieces.append(piece)
            row_map.append((held[0], first, n))
        ranges = [(sum(cuts[:i]), n) for i, n in enumerate(cuts)]
        run = feed_forward(code_map, row_map, ranges, depth, width, local_ff, weights is None)
        if weights is None:
            return tuple(run(ids, sidx, scale_table, *sources, *pieces, down_weight))
        return tuple(run(ids, sidx, scale_table, *pieces, *weights))

    def whole(mine, sibling):
        return (mine, 0, count), (sibling, 0, count)

    def halves(p):
        return [
            ((mine, p * h_rows, h_rows), (sibling, p * h_rows, h_rows))
            for mine, sibling in ((x_top, o_top), (x_low, o_low))
        ]

    def add(*terms):
        total = terms[0].astype(F32)
        for term in terms[1:]:
            total = total + term.astype(F32)
        return total

    o_top, o_low, o_right_z, o_left_z = swap(x_top, x_low, tbz, taz)
    later = after((tb, ta, tz, tokens), o_top, o_low)
    o_right, o_left, o_z, o_own = swap(*later)
    part = sums(ids, halves(1) + [whole(tbz, o_right_z), whole(taz, o_left_z)], [count] * 6)
    part, weights = part[:6], part[6:]
    part = after(part, o_right, o_left, o_z, o_own)
    got = swap(*part[3:])
    far_z, right, left = (add(part[i], got[i]).astype(BF16) for i in range(3))
    far_in, z_right, z_left = move(far_z, zh=1), move(right, dx=1), move(left, dx=-1)

    ids = after(ids, far_z, right, left)
    groups = halves(0) + [whole(tb, o_right), whole(ta, o_left), whole(tz, o_z)]
    part = sums(ids, groups, [h_rows] * 2 + [count] * 3 + [h_rows] * 2 + [count] * 3, weights)
    part, weights = part[:10], part[10:]
    far, near, here_z, near_sib, z_sib = part[:2], part[2:4], part[4], part[7:9], part[9]
    got = swap(*part[5:7])
    far, got, far_in, z_right, z_left = after((far, got, far_in, z_right, z_left))
    top = add(far[0], got[0], far_in[:h_rows]).astype(BF16)
    low = add(far[1], got[1], far_in[h_rows:]).astype(BF16)
    past_top, past_low = move(top, dx=1), move(low, dx=-1)

    near_sib, z_sib = after((near_sib, z_sib), top, low)
    got = swap(*near_sib, z_sib)
    right, left = add(near[0], got[0]), add(near[1], got[1])
    across = add(here_z, got[2], z_right, z_left).astype(BF16)
    ids = after(ids, top, low, right, left, across)
    here, own_sib = sums(ids, [whole(tokens, o_own)], [count] * 2, weights)[:2]
    right, left, across, past_top, past_low, here = after((right, left, across, past_top, past_low, here))
    zero = jnp.zeros((), BF16)
    past_top = lax.pad(past_top, zero, ((0, h_rows, 0), (0, 0, 0)))
    past_low = lax.pad(past_low, zero, ((h_rows, 0, 0), (0, 0, 0)))
    right, left = add(right, past_top).astype(BF16), add(left, past_low).astype(BF16)
    right_in, left_in, across_in = move(right, dx=1), move(left, dx=-1), move(across, zh=1)
    own_sib = after(own_sib, right, left, across)
    base = after(add(here, *swap(own_sib), across_in))
    return add(base, right_in, left_in).astype(BF16)


def solution(mesh):
    return jax.shard_map(
        body,
        mesh=mesh,
        in_specs=(
            P(("dp", "tensor"), None),
            P(("dp", "tensor"), None, None),
            P(("dp", "tensor")),
            P(("dp", "tensor")),
            P(),
            P("tensor", None),
        ),
        out_specs=P(("dp", "tensor"), None),
        check_vma=False,
    )
```

```python
import jax
import jax.numpy as jnp
from jax import lax
from jax.experimental import pallas as pl
from jax.experimental.pallas import tpu as pltpu
from jax.sharding import PartitionSpec as P

NX, NY, NZL, NZH, NC = 4, 4, 2, 2, 2
AXES = ("dp", "tensor")
BF16, F32 = jnp.bfloat16, jnp.float32
NOTE = 16
STEP = 2560


def place(y, zl, zh, x, c):
    return ((y % NY * NZL + zl % NZL) * NZH + zh % NZH) * NX * NC + x % NX * NC + c % NC


def move(value, dx=0, dy=0, zl=0, zh=0, core=0):
    pairs = []
    for y in range(NY):
        for l in range(NZL):
            for h in range(NZH):
                for x in range(NX):
                    for c in range(NC):
                        pairs.append((place(y, l, h, x, c), place(y + dy, l + zl, h + zh, x + dx, c + core)))
    return lax.ppermute(value, AXES, pairs)


def after(value, *others):
    return lax.optimization_barrier((value,) + others)[0]


def rows_of(*parts):
    return jnp.concatenate(parts, axis=0)


def with_note(codes, block_ids, scale_idx):
    _, depth, width = codes.shape

    def kernel(number, entry, block, out, note, sem):
        big = pltpu.make_async_copy(block.at[0], out.at[pl.ds(0, depth)], sem.at[0])
        big.start()
        line = lax.broadcasted_iota(jnp.int32, (NOTE, width), 0)
        note[...] = jnp.where(line == 0, number[0], entry[0]).astype(F32).astype(BF16)
        small = pltpu.make_async_copy(note, out.at[pl.ds(depth, NOTE)], sem.at[1])
        small.start()
        small.wait()
        big.wait()

    smem = pl.BlockSpec(memory_space=pltpu.SMEM)
    anywhere = pl.BlockSpec(memory_space=pltpu.HBM)
    return pl.pallas_call(
        kernel,
        out_shape=jax.ShapeDtypeStruct((depth + NOTE, width), BF16),
        in_specs=[smem, smem, anywhere],
        out_specs=anywhere,
        scratch_shapes=[pltpu.VMEM((NOTE, width), BF16), pltpu.SemaphoreType.DMA((2,))],
        compiler_params=pltpu.CompilerParams(vmem_limit_bytes=2 * 2**20),
    )(block_ids, scale_idx, codes)


def join(pieces, plans):
    n_copies = sum(len(plan) for plan in plans)

    def kernel(*refs):
        sources, outs, sem = refs[: len(pieces)], refs[len(pieces) : -1], refs[-1]
        copies = []
        for plan, out in zip(plans, outs):
            at = 0
            for src, first, n in plan:
                copies.append(
                    pltpu.make_async_copy(sources[src].at[pl.ds(first, n)], out.at[pl.ds(at, n)], sem.at[len(copies)])
                )
                at += n
        for c in copies:
            c.start()
        for c in copies:
            c.wait()

    anywhere = pl.BlockSpec(memory_space=pl.ANY)
    return pl.pallas_call(
        kernel,
        out_shape=tuple(
            jax.ShapeDtypeStruct((sum(n for _, _, n in plan), pieces[plan[0][0]].shape[1]), BF16) for plan in plans
        ),
        in_specs=[anywhere] * len(pieces),
        out_specs=(anywhere,) * len(plans),
        scratch_shapes=[pltpu.SemaphoreType.DMA((n_copies,))],
        compiler_params=pltpu.CompilerParams(vmem_limit_bytes=2 * 2**20),
        cost_estimate=pl.CostEstimate(flops=1, bytes_accessed=1, transcendentals=0),
    )(*pieces)


def feed_forward(code_map, row_map, ranges, depth, width, local_ff, load):
    n_codes = 1 + max(m[1] for m in code_map) if load else 0
    n_rows = 1 + max(m[0] for m in row_map)
    slots = 1 + max(m[0] for m in code_map)
    blocks = slots // 2
    rows = sum(m[2] for m in row_map)
    tile = rows if rows <= 576 else rows // 2
    n_out = len(ranges)
    base = len(code_map) + len(row_map)
    n_copies = base + 1 + 2 * n_out

    def kernel(ids, sidx, table, *refs):
        sources, refs = refs[:n_codes], refs[n_codes:]
        pieces, refs = refs[:n_rows], refs[n_rows:]
        if load:
            down, outs, (w, dn, x, proj, hid, out, sem) = refs[0], refs[1 : 1 + n_out], refs[1 + n_out :]
        else:
            w, dn, outs, (_, _, x, proj, hid, out, sem) = refs[0], refs[1], refs[2 : 2 + n_out], refs[2 + n_out :]
        at = 0
        tiles = [[] for _ in range(rows // tile)]
        for i, (src, start, n) in enumerate(row_map):
            copy = pltpu.make_async_copy(pieces[src].at[pl.ds(start, n)], x.at[pl.ds(at, n)], sem.at[i])
            tiles[at // tile].append(copy)
            at += n
        x_copies = [c for copies in tiles for c in copies]
        if load:
            waits = [[] for _ in range(blocks)]
            for i, (slot, src, start, n, to) in enumerate(code_map):
                target = w.at[slot // 2, pl.ds(to, n), pl.ds(slot % 2 * width, width)]
                waits[slot // 2].append(
                    pltpu.make_async_copy(sources[src].at[pl.ds(start, n)], target, sem.at[len(row_map) + i])
                )
            down_copy = pltpu.make_async_copy(down, dn, sem.at[n_copies - 1])
            stages = [x_copies + waits[0]] + waits[1:] + [[down_copy]]
            for stage in stages[:2]:
                for c in stage:
                    c.start()
        else:
            for c in x_copies:
                c.start()
        for c in tiles[0]:
            c.wait()

        @pl.loop(0, blocks)
        def _(pair):
            if load:
                for q in range(blocks):

                    @pl.when(pair == q)
                    def _(q=q):
                        for c in waits[q]:
                            c.wait()
                        if q + 2 < len(stages):
                            for c in stages[q + 2]:
                                c.start()

            @pl.loop(0, rows // tile)
            def _(part):
                for t in range(1, rows // tile):

                    @pl.when((pair == 0) & (part == t))
                    def _(t=t):
                        for c in tiles[t]:
                            c.wait()

                at = pl.ds(pl.multiple_of(part * tile, tile), tile)
                acc = jnp.dot(x[at, :], w[pair], preferred_element_type=F32)
                for side in range(2):
                    slot = 2 * pair + side
                    proj[ids[slot], at] = acc[:, side * width : (side + 1) * width] * table[sidx[slot]]

        @pl.loop(0, rows // tile)
        def _(part):
            at = pl.ds(pl.multiple_of(part * tile, tile), tile)
            for b in range(blocks):
                gate, up = proj[b, at], proj[b + blocks, at]
                hid[at, b * width : (b + 1) * width] = (gate / (1.0 + jnp.exp(-gate)) * up).astype(BF16)

        if load:
            down_copy.wait()

        def leave(n, slot):
            cols = pl.ds(pl.multiple_of(n * STEP, STEP), STEP)
            return [
                pltpu.make_async_copy(out.at[slot, pl.ds(at, n)], outs[i].at[:, cols], sem.at[base + slot * n_out + i])
                for i, (at, n) in enumerate(ranges)
            ]

        steps = depth // STEP

        @pl.loop(0, steps)
        def _(n):
            slot = lax.rem(n, 2)

            @pl.when(n >= 2)
            def _():
                for c in leave(n - 2, slot):
                    c.wait()

            cols = pl.ds(pl.multiple_of(n * STEP, STEP), STEP)

            @pl.loop(0, rows // tile)
            def _(part):
                at = pl.ds(pl.multiple_of(part * tile, tile), tile)
                out[slot, at] = jnp.dot(hid[at, :], dn[:, cols], preferred_element_type=F32).astype(BF16)

            for c in leave(n, slot):
                c.start()

        for n in (steps - 2, steps - 1):
            for c in leave(n, n % 2):
                c.wait()

    anywhere = pl.BlockSpec(memory_space=pltpu.HBM)
    smem = pl.BlockSpec(memory_space=pltpu.SMEM)
    vmem = pl.BlockSpec(memory_space=pltpu.VMEM)
    results = tuple(jax.ShapeDtypeStruct((n, depth), BF16) for _, n in ranges)
    kept = (pltpu.VMEM((blocks, depth, 2 * width), BF16), pltpu.VMEM((local_ff, depth), BF16))
    return pl.pallas_call(
        kernel,
        out_shape=results + kept,
        in_specs=[smem] * 3 + [anywhere] * (n_codes + n_rows) + ([anywhere] if load else [vmem, vmem]),
        out_specs=(anywhere,) * n_out + (vmem, vmem),
        input_output_aliases={} if load else {3 + n_rows: n_out, 4 + n_rows: n_out + 1},
        scratch_shapes=[
            pltpu.VMEM((rows, depth), BF16),
            pltpu.VMEM((slots, rows, width), F32),
            pltpu.VMEM((rows, local_ff), BF16),
            pltpu.VMEM((2, rows, STEP), BF16),
            pltpu.SemaphoreType.DMA((n_copies,)),
        ],
        compiler_params=pltpu.CompilerParams(vmem_limit_bytes=44 * 2**20),
        cost_estimate=pl.CostEstimate(
            flops=2 * rows * depth * local_ff * 3,
            bytes_accessed=2 * (depth * slots * width + local_ff * depth + 2 * rows * depth),
            transcendentals=rows * local_ff,
        ),
    )


def body(tokens, codes, block_ids, scale_idx, scale_table, down_weight):
    count, depth = tokens.shape
    width = codes.shape[2]
    local_ff = down_weight.shape[0]
    h_rows, h_depth = count // 2, depth // 2

    own = with_note(codes, block_ids, scale_idx)
    ca, cb = move(own, dy=1), move(own, dy=-1)
    ta, tb, tz = move(tokens, dx=1), move(tokens, dx=-1), move(tokens, zh=1)
    cz = move(after(own, tz), zl=1)
    y_top = move(rows_of(ca[:h_depth], ca[depth:]), dy=1)
    y_low = move(cb[h_depth:depth], dy=-1)
    tz_x = after(tz, ta, tb)
    taz, tbz = move(tz_x, dx=1), move(tz_x, dx=-1)
    cy, top_in, low_in = join(
        (y_top, y_low, ta, taz, tb, tbz),
        (
            ((0, 0, h_depth), (1, 0, h_depth), (0, h_depth, NOTE)),
            ((2, 0, h_rows), (3, 0, h_rows)),
            ((4, h_rows, h_rows), (5, h_rows, h_rows)),
        ),
    )
    cy, cz_y = after((cy, cz), top_in)
    caz, cbz, cyz = move(cz_y, dy=1), move(cz_y, dy=-1), move(cy, zl=1)
    x_top, x_low = move(top_in, dx=1), move(low_in, dx=-1)

    sources = [own, ca, cb, cz, cy, caz, cbz, cyz]
    code_map = [(i, i, 0, depth, 0) for i in range(8)]
    notes = jnp.stack([s[depth : depth + 2, 0] for s in sources]).astype(jnp.int32)
    ids, sidx = notes[:, 0], notes[:, 1]

    def swap(*pieces):
        return tuple(move(piece, core=1) for piece in pieces)

    def sums(ids, groups, cuts, weights=None):
        pieces, row_map = [], []
        for piece, first, n in [g[0] for g in groups] + [g[1] for g in groups]:
            held = [i for i, p in enumerate(pieces) if p is piece]
            if not held:
                held = [len(pieces)]
                pieces.append(piece)
            row_map.append((held[0], first, n))
        ranges = [(sum(cuts[:i]), n) for i, n in enumerate(cuts)]
        run = feed_forward(code_map, row_map, ranges, depth, width, local_ff, weights is None)
        if weights is None:
            return tuple(run(ids, sidx, scale_table, *sources, *pieces, down_weight))
        return tuple(run(ids, sidx, scale_table, *pieces, *weights))

    def whole(mine, sibling):
        return (mine, 0, count), (sibling, 0, count)

    def halves(p):
        return [
            ((mine, p * h_rows, h_rows), (sibling, p * h_rows, h_rows))
            for mine, sibling in ((x_top, o_top), (x_low, o_low))
        ]

    def add(*terms):
        total = terms[0].astype(F32)
        for term in terms[1:]:
            total = total + term.astype(F32)
        return total

    o_top, o_low, o_right_z, o_left_z = swap(x_top, x_low, tbz, taz)
    later = after((tb, ta, tz, tokens), o_top, o_low)
    o_right, o_left, o_z, o_own = swap(*later)
    part = sums(ids, halves(1) + [whole(tbz, o_right_z), whole(taz, o_left_z)], [count] * 6)
    part, weights = part[:6], part[6:]
    part = after(part, o_right, o_left, o_z, o_own)
    got = swap(*part[3:])
    far_z, right, left = (add(part[i], got[i]).astype(BF16) for i in range(3))
    far_in, z_right, z_left = move(far_z, zh=1), move(right, dx=1), move(left, dx=-1)

    ids = after(ids, far_z, right, left)
    groups = halves(0) + [whole(tb, o_right), whole(ta, o_left), whole(tz, o_z)]
    part = sums(ids, groups, [h_rows] * 2 + [count] * 3 + [h_rows] * 2 + [count] * 3, weights)
    part, weights = part[:10], part[10:]
    far, near, here_z, near_sib, z_sib = part[:2], part[2:4], part[4], part[7:9], part[9]
    got = swap(*part[5:7])
    far, got, far_in, z_right, z_left = after((far, got, far_in, z_right, z_left))
    top = add(far[0], got[0], far_in[:h_rows]).astype(BF16)
    low = add(after(far[1], top), got[1], far_in[h_rows:]).astype(BF16)
    past_top, past_low = move(top, dx=1), move(low, dx=-1)

    near_sib, z_sib = after((near_sib, z_sib), top, low)
    got = swap(*near_sib, z_sib)
    right, left = add(near[0], got[0]), add(near[1], got[1])
    across = add(here_z, got[2], z_right, z_left).astype(BF16)
    ids = after(ids, top, low, right, left, across)
    here, own_sib = sums(ids, [whole(tokens, o_own)], [count] * 2, weights)[:2]
    right, left, across, past_top, past_low, here = after((right, left, across, past_top, past_low, here))
    zero = jnp.zeros((), BF16)
    past_top = lax.pad(past_top, zero, ((0, h_rows, 0), (0, 0, 0)))
    past_low = lax.pad(past_low, zero, ((h_rows, 0, 0), (0, 0, 0)))
    right, left = add(right, past_top).astype(BF16), add(left, past_low).astype(BF16)
    right_in, left_in, across_in = move(right, dx=1), move(left, dx=-1), move(across, zh=1)
    own_sib = after(own_sib, right, left, across)
    base = after(add(here, *swap(own_sib), across_in))
    return add(base, right_in, left_in).astype(BF16)


def solution(mesh):
    return jax.shard_map(
        body,
        mesh=mesh,
        in_specs=(
            P(("dp", "tensor"), None),
            P(("dp", "tensor"), None, None),
            P(("dp", "tensor")),
            P(("dp", "tensor")),
            P(),
            P("tensor", None),
        ),
        out_specs=P(("dp", "tensor"), None),
        check_vma=False,
    )
```

```python
import jax
import jax.numpy as jnp
from jax import lax
from jax.experimental import pallas as pl
from jax.experimental.pallas import tpu as pltpu
from jax.sharding import PartitionSpec as P

NX, NY, NZL, NZH, NC = 4, 4, 2, 2, 2
AXES = ("dp", "tensor")
BF16, F32 = jnp.bfloat16, jnp.float32
NOTE = 16
STEP = 2560


def place(y, zl, zh, x, c):
    return ((y % NY * NZL + zl % NZL) * NZH + zh % NZH) * NX * NC + x % NX * NC + c % NC


def move(value, dx=0, dy=0, zl=0, zh=0, core=0):
    pairs = []
    for y in range(NY):
        for l in range(NZL):
            for h in range(NZH):
                for x in range(NX):
                    for c in range(NC):
                        pairs.append((place(y, l, h, x, c), place(y + dy, l + zl, h + zh, x + dx, c + core)))
    return lax.ppermute(value, AXES, pairs)


def after(value, *others):
    return lax.optimization_barrier((value,) + others)[0]


def rows_of(*parts):
    return jnp.concatenate(parts, axis=0)


def with_note(codes, block_ids, scale_idx):
    _, depth, width = codes.shape

    def kernel(number, entry, block, out, note, sem):
        big = pltpu.make_async_copy(block.at[0], out.at[pl.ds(0, depth)], sem.at[0])
        big.start()
        line = lax.broadcasted_iota(jnp.int32, (NOTE, width), 0)
        note[...] = jnp.where(line == 0, number[0], entry[0]).astype(F32).astype(BF16)
        small = pltpu.make_async_copy(note, out.at[pl.ds(depth, NOTE)], sem.at[1])
        small.start()
        small.wait()
        big.wait()

    smem = pl.BlockSpec(memory_space=pltpu.SMEM)
    anywhere = pl.BlockSpec(memory_space=pltpu.HBM)
    return pl.pallas_call(
        kernel,
        out_shape=jax.ShapeDtypeStruct((depth + NOTE, width), BF16),
        in_specs=[smem, smem, anywhere],
        out_specs=anywhere,
        scratch_shapes=[pltpu.VMEM((NOTE, width), BF16), pltpu.SemaphoreType.DMA((2,))],
        compiler_params=pltpu.CompilerParams(vmem_limit_bytes=2 * 2**20),
    )(block_ids, scale_idx, codes)


def join(pieces, plans):
    n_copies = sum(len(plan) for plan in plans)

    def kernel(*refs):
        sources, outs, sem = refs[: len(pieces)], refs[len(pieces) : -1], refs[-1]
        copies = []
        for plan, out in zip(plans, outs):
            at = 0
            for src, first, n in plan:
                copies.append(
                    pltpu.make_async_copy(sources[src].at[pl.ds(first, n)], out.at[pl.ds(at, n)], sem.at[len(copies)])
                )
                at += n
        for c in copies:
            c.start()
        for c in copies:
            c.wait()

    anywhere = pl.BlockSpec(memory_space=pl.ANY)
    return pl.pallas_call(
        kernel,
        out_shape=tuple(
            jax.ShapeDtypeStruct((sum(n for _, _, n in plan), pieces[plan[0][0]].shape[1]), BF16) for plan in plans
        ),
        in_specs=[anywhere] * len(pieces),
        out_specs=(anywhere,) * len(plans),
        scratch_shapes=[pltpu.SemaphoreType.DMA((n_copies,))],
        compiler_params=pltpu.CompilerParams(vmem_limit_bytes=2 * 2**20),
        cost_estimate=pl.CostEstimate(flops=1, bytes_accessed=1, transcendentals=0),
    )(*pieces)


def feed_forward(code_map, row_map, ranges, depth, width, local_ff, load):
    n_codes = 1 + max(m[1] for m in code_map) if load else 0
    n_rows = 1 + max(m[0] for m in row_map)
    slots = 1 + max(m[0] for m in code_map)
    blocks = slots // 2
    rows = sum(m[2] for m in row_map)
    tile = rows if rows <= 576 else rows // 2
    n_out = len(ranges)
    base = len(code_map) + len(row_map)
    n_copies = base + 1 + 2 * n_out

    def kernel(ids, sidx, table, *refs):
        sources, refs = refs[:n_codes], refs[n_codes:]
        pieces, refs = refs[:n_rows], refs[n_rows:]
        if load:
            down, outs, (w, dn, x, proj, hid, out, sem) = refs[0], refs[1 : 1 + n_out], refs[1 + n_out :]
        else:
            w, dn, outs, (_, _, x, proj, hid, out, sem) = refs[0], refs[1], refs[2 : 2 + n_out], refs[2 + n_out :]
        at = 0
        tiles = [[] for _ in range(rows // tile)]
        for i, (src, start, n) in enumerate(row_map):
            copy = pltpu.make_async_copy(pieces[src].at[pl.ds(start, n)], x.at[pl.ds(at, n)], sem.at[i])
            tiles[at // tile].append(copy)
            at += n
        x_copies = [c for copies in tiles for c in copies]
        if load:
            waits = [[] for _ in range(blocks)]
            for i, (slot, src, start, n, to) in enumerate(code_map):
                target = w.at[slot // 2, pl.ds(to, n), pl.ds(slot % 2 * width, width)]
                waits[slot // 2].append(
                    pltpu.make_async_copy(sources[src].at[pl.ds(start, n)], target, sem.at[len(row_map) + i])
                )
            down_copy = pltpu.make_async_copy(down, dn, sem.at[n_copies - 1])
            stages = [x_copies + waits[0]] + waits[1:] + [[down_copy]]
            for stage in stages[:2]:
                for c in stage:
                    c.start()
        else:
            for c in x_copies:
                c.start()
        for c in tiles[0]:
            c.wait()

        @pl.loop(0, blocks)
        def _(pair):
            if load:
                for q in range(blocks):

                    @pl.when(pair == q)
                    def _(q=q):
                        for c in waits[q]:
                            c.wait()
                        if q + 2 < len(stages):
                            for c in stages[q + 2]:
                                c.start()

            @pl.loop(0, rows // tile)
            def _(part):
                for t in range(1, rows // tile):

                    @pl.when((pair == 0) & (part == t))
                    def _(t=t):
                        for c in tiles[t]:
                            c.wait()

                at = pl.ds(pl.multiple_of(part * tile, tile), tile)
                acc = jnp.dot(x[at, :], w[pair], preferred_element_type=F32)
                for side in range(2):
                    slot = 2 * pair + side
                    proj[ids[slot], at] = acc[:, side * width : (side + 1) * width] * table[sidx[slot]]

        @pl.loop(0, rows // tile)
        def _(part):
            at = pl.ds(pl.multiple_of(part * tile, tile), tile)
            for b in range(blocks):
                gate, up = proj[b, at], proj[b + blocks, at]
                hid[at, b * width : (b + 1) * width] = (gate / (1.0 + jnp.exp(-gate)) * up).astype(BF16)

        if load:
            down_copy.wait()

        def leave(n, slot):
            cols = pl.ds(pl.multiple_of(n * STEP, STEP), STEP)
            return [
                pltpu.make_async_copy(out.at[slot, pl.ds(at, n)], outs[i].at[:, cols], sem.at[base + slot * n_out + i])
                for i, (at, n) in enumerate(ranges)
            ]

        steps = depth // STEP

        @pl.loop(0, steps)
        def _(n):
            slot = lax.rem(n, 2)

            @pl.when(n >= 2)
            def _():
                for c in leave(n - 2, slot):
                    c.wait()

            cols = pl.ds(pl.multiple_of(n * STEP, STEP), STEP)

            @pl.loop(0, rows // tile)
            def _(part):
                at = pl.ds(pl.multiple_of(part * tile, tile), tile)
                out[slot, at] = jnp.dot(hid[at, :], dn[:, cols], preferred_element_type=F32).astype(BF16)

            for c in leave(n, slot):
                c.start()

        for n in (steps - 2, steps - 1):
            for c in leave(n, n % 2):
                c.wait()

    anywhere = pl.BlockSpec(memory_space=pltpu.HBM)
    smem = pl.BlockSpec(memory_space=pltpu.SMEM)
    vmem = pl.BlockSpec(memory_space=pltpu.VMEM)
    results = tuple(jax.ShapeDtypeStruct((n, depth), BF16) for _, n in ranges)
    kept = (pltpu.VMEM((blocks, depth, 2 * width), BF16), pltpu.VMEM((local_ff, depth), BF16))
    return pl.pallas_call(
        kernel,
        out_shape=results + kept,
        in_specs=[smem] * 3 + [anywhere] * (n_codes + n_rows) + ([anywhere] if load else [vmem, vmem]),
        out_specs=(anywhere,) * n_out + (vmem, vmem),
        input_output_aliases={} if load else {3 + n_rows: n_out, 4 + n_rows: n_out + 1},
        scratch_shapes=[
            pltpu.VMEM((rows, depth), BF16),
            pltpu.VMEM((slots, rows, width), F32),
            pltpu.VMEM((rows, local_ff), BF16),
            pltpu.VMEM((2, rows, STEP), BF16),
            pltpu.SemaphoreType.DMA((n_copies,)),
        ],
        compiler_params=pltpu.CompilerParams(vmem_limit_bytes=44 * 2**20),
        cost_estimate=pl.CostEstimate(
            flops=2 * rows * depth * local_ff * 3,
            bytes_accessed=2 * (depth * slots * width + local_ff * depth + 2 * rows * depth),
            transcendentals=rows * local_ff,
        ),
    )


def body(tokens, codes, block_ids, scale_idx, scale_table, down_weight):
    count, depth = tokens.shape
    width = codes.shape[2]
    local_ff = down_weight.shape[0]
    h_rows, h_depth = count // 2, depth // 2

    own = with_note(codes, block_ids, scale_idx)
    ca, cb = move(own, dy=1), move(own, dy=-1)
    ta, tb, tz = move(tokens, dx=1), move(tokens, dx=-1), move(tokens, zh=1)
    cz = move(after(own, tz), zl=1)
    y_top = move(rows_of(ca[:h_depth], ca[depth:]), dy=1)
    y_low = move(cb[h_depth:depth], dy=-1)
    tz_x = after(tz, ta, tb)
    taz, tbz = move(tz_x, dx=1), move(tz_x, dx=-1)
    cy, top_in, low_in = join(
        (y_top, y_low, ta, taz, tb, tbz),
        (
            ((0, 0, h_depth), (1, 0, h_depth), (0, h_depth, NOTE)),
            ((2, 0, h_rows), (3, 0, h_rows)),
            ((4, h_rows, h_rows), (5, h_rows, h_rows)),
        ),
    )
    cy, cz_y = after((cy, cz), top_in)
    caz, cbz, cyz = move(cz_y, dy=1), move(cz_y, dy=-1), move(cy, zl=1)
    x_top, x_low = move(top_in, dx=1), move(low_in, dx=-1)

    sources = [own, ca, cb, cz, cy, caz, cbz, cyz]
    code_map = [(i, i, 0, depth, 0) for i in range(8)]
    notes = jnp.stack([s[depth : depth + 2, 0] for s in sources]).astype(jnp.int32)
    ids, sidx = notes[:, 0], notes[:, 1]

    def swap(*pieces):
        return tuple(move(piece, core=1) for piece in pieces)

    def sums(ids, groups, cuts, weights=None):
        pieces, row_map = [], []
        for piece, first, n in [g[0] for g in groups] + [g[1] for g in groups]:
            held = [i for i, p in enumerate(pieces) if p is piece]
            if not held:
                held = [len(pieces)]
                pieces.append(piece)
            row_map.append((held[0], first, n))
        ranges = [(sum(cuts[:i]), n) for i, n in enumerate(cuts)]
        run = feed_forward(code_map, row_map, ranges, depth, width, local_ff, weights is None)
        if weights is None:
            return tuple(run(ids, sidx, scale_table, *sources, *pieces, down_weight))
        return tuple(run(ids, sidx, scale_table, *pieces, *weights))

    def whole(mine, sibling):
        return (mine, 0, count), (sibling, 0, count)

    def halves(p):
        return [
            ((mine, p * h_rows, h_rows), (sibling, p * h_rows, h_rows))
            for mine, sibling in ((x_top, o_top), (x_low, o_low))
        ]

    def add(*terms):
        total = terms[0].astype(F32)
        for term in terms[1:]:
            total = total + term.astype(F32)
        return total

    o_top, o_low, o_right_z, o_left_z = swap(x_top, x_low, tbz, taz)
    later = after((tb, ta, tz, tokens), o_top, o_low)
    o_right, o_left, o_z, o_own = swap(*later)
    part = sums(ids, halves(1) + [whole(tbz, o_right_z), whole(taz, o_left_z)], [count] * 6)
    part, weights = part[:6], part[6:]
    part = after(part, o_right, o_left, o_z, o_own)
    got = swap(*part[3:])
    far_z, right, left = (add(part[i], got[i]).astype(BF16) for i in range(3))
    far_in, z_right, z_left = move(far_z, zh=1), move(right, dx=1), move(left, dx=-1)

    ids = after(ids, far_z, right, left)
    groups = halves(0) + [whole(tb, o_right), whole(ta, o_left), whole(tz, o_z)]
    part = sums(ids, groups, [h_rows] * 2 + [count] * 3 + [h_rows] * 2 + [count] * 3, weights)
    part, weights = part[:10], part[10:]
    far, near, here_z, near_sib, z_sib = part[:2], part[2:4], part[4], part[7:9], part[9]
    got = swap(*part[5:7])
    far, got, far_in, z_right, z_left = after((far, got, far_in, z_right, z_left))
    top = add(far[0], got[0], far_in[:h_rows]).astype(BF16)
    low = add(far[1], got[1], far_in[h_rows:]).astype(BF16)
    past_top, past_low = move(top, dx=1), move(low, dx=-1)

    near_sib, z_sib = after((near_sib, z_sib), top, low)
    got = swap(*near_sib, z_sib)
    right, left = add(near[0], got[0]), add(near[1], got[1])
    across = add(here_z, got[2], z_right, z_left).astype(BF16)
    ids = after(ids, top, low, right, left, across)
    here, own_sib = sums(ids, [whole(tokens, o_own)], [count] * 2, weights)[:2]
    right, left, across, past_top, past_low, here = after((right, left, across, past_top, past_low, here))
    zero = jnp.zeros((), BF16)
    past_top = lax.pad(past_top, zero, ((0, h_rows, 0), (0, 0, 0)))
    past_low = lax.pad(past_low, zero, ((h_rows, 0, 0), (0, 0, 0)))
    right, left = add(right, past_top).astype(BF16), add(left, past_low).astype(BF16)
    right_in, left_in, across_in = move(right, dx=1), move(left, dx=-1), move(across, zh=1)
    own_sib = after(own_sib, right, left, across)
    base = after(add(here, *swap(own_sib), across_in))
    return add(base, right_in, left_in).astype(BF16)


def solution(mesh):
    return jax.shard_map(
        body,
        mesh=mesh,
        in_specs=(
            P(("dp", "tensor"), None),
            P(("dp", "tensor"), None, None),
            P(("dp", "tensor")),
            P(("dp", "tensor")),
            P(),
            P("tensor", None),
        ),
        out_specs=P(("dp", "tensor"), None),
        check_vma=False,
    )
```

```python
import jax
import jax.numpy as jnp
from jax import lax
from jax.experimental import pallas as pl
from jax.experimental.pallas import tpu as pltpu
from jax.sharding import PartitionSpec as P

NX, NY, NZL, NZH, NC = 4, 4, 2, 2, 2
AXES = ("dp", "tensor")
BF16, F32 = jnp.bfloat16, jnp.float32
NOTE = 16
STEP = 2560


def place(y, zl, zh, x, c):
    return ((y % NY * NZL + zl % NZL) * NZH + zh % NZH) * NX * NC + x % NX * NC + c % NC


def move(value, dx=0, dy=0, zl=0, zh=0, core=0):
    pairs = []
    for y in range(NY):
        for l in range(NZL):
            for h in range(NZH):
                for x in range(NX):
                    for c in range(NC):
                        pairs.append((place(y, l, h, x, c), place(y + dy, l + zl, h + zh, x + dx, c + core)))
    return lax.ppermute(value, AXES, pairs)


def after(value, *others):
    return lax.optimization_barrier((value,) + others)[0]


def rows_of(*parts):
    return jnp.concatenate(parts, axis=0)


def with_note(codes, block_ids, scale_idx):
    _, depth, width = codes.shape

    def kernel(number, entry, block, out, note, sem):
        big = pltpu.make_async_copy(block.at[0], out.at[pl.ds(0, depth)], sem.at[0])
        big.start()
        line = lax.broadcasted_iota(jnp.int32, (NOTE, width), 0)
        note[...] = jnp.where(line == 0, number[0], entry[0]).astype(F32).astype(BF16)
        small = pltpu.make_async_copy(note, out.at[pl.ds(depth, NOTE)], sem.at[1])
        small.start()
        small.wait()
        big.wait()

    smem = pl.BlockSpec(memory_space=pltpu.SMEM)
    anywhere = pl.BlockSpec(memory_space=pltpu.HBM)
    return pl.pallas_call(
        kernel,
        out_shape=jax.ShapeDtypeStruct((depth + NOTE, width), BF16),
        in_specs=[smem, smem, anywhere],
        out_specs=anywhere,
        scratch_shapes=[pltpu.VMEM((NOTE, width), BF16), pltpu.SemaphoreType.DMA((2,))],
        compiler_params=pltpu.CompilerParams(vmem_limit_bytes=2 * 2**20),
    )(block_ids, scale_idx, codes)


def join(pieces, plans):
    n_copies = sum(len(plan) for plan in plans)

    def kernel(*refs):
        sources, outs, sem = refs[: len(pieces)], refs[len(pieces) : -1], refs[-1]
        copies = []
        for plan, out in zip(plans, outs):
            at = 0
            for src, first, n in plan:
                copies.append(
                    pltpu.make_async_copy(sources[src].at[pl.ds(first, n)], out.at[pl.ds(at, n)], sem.at[len(copies)])
                )
                at += n
        for c in copies:
            c.start()
        for c in copies:
            c.wait()

    anywhere = pl.BlockSpec(memory_space=pl.ANY)
    return pl.pallas_call(
        kernel,
        out_shape=tuple(
            jax.ShapeDtypeStruct((sum(n for _, _, n in plan), pieces[plan[0][0]].shape[1]), BF16) for plan in plans
        ),
        in_specs=[anywhere] * len(pieces),
        out_specs=(anywhere,) * len(plans),
        scratch_shapes=[pltpu.SemaphoreType.DMA((n_copies,))],
        compiler_params=pltpu.CompilerParams(vmem_limit_bytes=2 * 2**20),
        cost_estimate=pl.CostEstimate(flops=1, bytes_accessed=1, transcendentals=0),
    )(*pieces)


def feed_forward(code_map, row_map, ranges, depth, width, local_ff, load):
    n_codes = 1 + max(m[1] for m in code_map) if load else 0
    n_rows = 1 + max(m[0] for m in row_map)
    slots = 1 + max(m[0] for m in code_map)
    blocks = slots // 2
    rows = sum(m[2] for m in row_map)
    tile = rows if rows <= 576 else rows // 2
    n_out = len(ranges)
    base = len(code_map) + len(row_map)
    n_copies = base + 1 + 2 * n_out

    def kernel(ids, sidx, table, *refs):
        sources, refs = refs[:n_codes], refs[n_codes:]
        pieces, refs = refs[:n_rows], refs[n_rows:]
        if load:
            down, outs, (w, dn, x, proj, hid, out, sem) = refs[0], refs[1 : 1 + n_out], refs[1 + n_out :]
        else:
            w, dn, outs, (_, _, x, proj, hid, out, sem) = refs[0], refs[1], refs[2 : 2 + n_out], refs[2 + n_out :]
        at = 0
        tiles = [[] for _ in range(rows // tile)]
        for i, (src, start, n) in enumerate(row_map):
            copy = pltpu.make_async_copy(pieces[src].at[pl.ds(start, n)], x.at[pl.ds(at, n)], sem.at[i])
            tiles[at // tile].append(copy)
            at += n
        x_copies = [c for copies in tiles for c in copies]
        if load:
            waits = [[] for _ in range(blocks)]
            for i, (slot, src, start, n, to) in enumerate(code_map):
                target = w.at[slot // 2, pl.ds(to, n), pl.ds(slot % 2 * width, width)]
                waits[slot // 2].append(
                    pltpu.make_async_copy(sources[src].at[pl.ds(start, n)], target, sem.at[len(row_map) + i])
                )
            down_copy = pltpu.make_async_copy(down, dn, sem.at[n_copies - 1])
            stages = [x_copies + waits[0]] + waits[1:] + [[down_copy]]
            for stage in stages[:2]:
                for c in stage:
                    c.start()
        else:
            for c in x_copies:
                c.start()
        for c in tiles[0]:
            c.wait()

        @pl.loop(0, blocks)
        def _(pair):
            if load:
                for q in range(blocks):

                    @pl.when(pair == q)
                    def _(q=q):
                        for c in waits[q]:
                            c.wait()
                        if q + 2 < len(stages):
                            for c in stages[q + 2]:
                                c.start()

            @pl.loop(0, rows // tile)
            def _(part):
                for t in range(1, rows // tile):

                    @pl.when((pair == 0) & (part == t))
                    def _(t=t):
                        for c in tiles[t]:
                            c.wait()

                at = pl.ds(pl.multiple_of(part * tile, tile), tile)
                acc = jnp.dot(x[at, :], w[pair], preferred_element_type=F32)
                for side in range(2):
                    slot = 2 * pair + side
                    proj[ids[slot], at] = acc[:, side * width : (side + 1) * width] * table[sidx[slot]]

        @pl.loop(0, rows // tile)
        def _(part):
            at = pl.ds(pl.multiple_of(part * tile, tile), tile)
            for b in range(blocks):
                gate, up = proj[b, at], proj[b + blocks, at]
                hid[at, b * width : (b + 1) * width] = (gate / (1.0 + jnp.exp(-gate)) * up).astype(BF16)

        if load:
            down_copy.wait()

        def leave(n, slot):
            cols = pl.ds(pl.multiple_of(n * STEP, STEP), STEP)
            return [
                pltpu.make_async_copy(out.at[slot, pl.ds(at, n)], outs[i].at[:, cols], sem.at[base + slot * n_out + i])
                for i, (at, n) in enumerate(ranges)
            ]

        steps = depth // STEP

        @pl.loop(0, steps)
        def _(n):
            slot = lax.rem(n, 2)

            @pl.when(n >= 2)
            def _():
                for c in leave(n - 2, slot):
                    c.wait()

            cols = pl.ds(pl.multiple_of(n * STEP, STEP), STEP)

            @pl.loop(0, rows // tile)
            def _(part):
                at = pl.ds(pl.multiple_of(part * tile, tile), tile)
                out[slot, at] = jnp.dot(hid[at, :], dn[:, cols], preferred_element_type=F32).astype(BF16)

            for c in leave(n, slot):
                c.start()

        for n in (steps - 2, steps - 1):
            for c in leave(n, n % 2):
                c.wait()

    anywhere = pl.BlockSpec(memory_space=pltpu.HBM)
    smem = pl.BlockSpec(memory_space=pltpu.SMEM)
    vmem = pl.BlockSpec(memory_space=pltpu.VMEM)
    results = tuple(jax.ShapeDtypeStruct((n, depth), BF16) for _, n in ranges)
    kept = (pltpu.VMEM((blocks, depth, 2 * width), BF16), pltpu.VMEM((local_ff, depth), BF16))
    return pl.pallas_call(
        kernel,
        out_shape=results + kept,
        in_specs=[smem] * 3 + [anywhere] * (n_codes + n_rows) + ([anywhere] if load else [vmem, vmem]),
        out_specs=(anywhere,) * n_out + (vmem, vmem),
        input_output_aliases={} if load else {3 + n_rows: n_out, 4 + n_rows: n_out + 1},
        scratch_shapes=[
            pltpu.VMEM((rows, depth), BF16),
            pltpu.VMEM((slots, rows, width), F32),
            pltpu.VMEM((rows, local_ff), BF16),
            pltpu.VMEM((2, rows, STEP), BF16),
            pltpu.SemaphoreType.DMA((n_copies,)),
        ],
        compiler_params=pltpu.CompilerParams(vmem_limit_bytes=36 * 2**20),
        cost_estimate=pl.CostEstimate(
            flops=2 * rows * depth * local_ff * 3,
            bytes_accessed=2 * (depth * slots * width + local_ff * depth + 2 * rows * depth),
            transcendentals=rows * local_ff,
        ),
    )


def body(tokens, codes, block_ids, scale_idx, scale_table, down_weight):
    count, depth = tokens.shape
    width = codes.shape[2]
    local_ff = down_weight.shape[0]
    h_rows, h_depth = count // 2, depth // 2

    own = with_note(codes, block_ids, scale_idx)
    ca, cb = move(own, dy=1), move(own, dy=-1)
    ta, tb, tz = move(tokens, dx=1), move(tokens, dx=-1), move(tokens, zh=1)
    cz = move(after(own, tz), zl=1)
    y_top = move(rows_of(ca[:h_depth], ca[depth:]), dy=1)
    y_low = move(cb[h_depth:depth], dy=-1)
    tz_x = after(tz, ta, tb)
    taz, tbz = move(tz_x, dx=1), move(tz_x, dx=-1)
    cy, top_in, low_in = join(
        (y_top, y_low, ta, taz, tb, tbz),
        (
            ((0, 0, h_depth), (1, 0, h_depth), (0, h_depth, NOTE)),
            ((2, 0, h_rows), (3, 0, h_rows)),
            ((4, h_rows, h_rows), (5, h_rows, h_rows)),
        ),
    )
    cy, cz_y = after((cy, cz), top_in)
    caz, cbz, cyz = move(cz_y, dy=1), move(cz_y, dy=-1), move(cy, zl=1)
    x_top, x_low = move(top_in, dx=1), move(low_in, dx=-1)

    sources = [own, ca, cb, cz, cy, caz, cbz, cyz]
    code_map = [(i, i, 0, depth, 0) for i in range(8)]
    notes = jnp.stack([s[depth : depth + 2, 0] for s in sources]).astype(jnp.int32)
    ids, sidx = notes[:, 0], notes[:, 1]

    def swap(*pieces):
        return tuple(move(piece, core=1) for piece in pieces)

    def sums(ids, groups, cuts, weights=None):
        pieces, row_map = [], []
        for piece, first, n in [g[0] for g in groups] + [g[1] for g in groups]:
            held = [i for i, p in enumerate(pieces) if p is piece]
            if not held:
                held = [len(pieces)]
                pieces.append(piece)
            row_map.append((held[0], first, n))
        ranges = [(sum(cuts[:i]), n) for i, n in enumerate(cuts)]
        run = feed_forward(code_map, row_map, ranges, depth, width, local_ff, weights is None)
        if weights is None:
            return tuple(run(ids, sidx, scale_table, *sources, *pieces, down_weight))
        return tuple(run(ids, sidx, scale_table, *pieces, *weights))

    def whole(mine, sibling):
        return (mine, 0, count), (sibling, 0, count)

    def halves(p):
        return [
            ((mine, p * h_rows, h_rows), (sibling, p * h_rows, h_rows))
            for mine, sibling in ((x_top, o_top), (x_low, o_low))
        ]

    def add(*terms):
        total = terms[0].astype(F32)
        for term in terms[1:]:
            total = total + term.astype(F32)
        return total

    o_top, o_low, o_right_z, o_left_z = swap(x_top, x_low, tbz, taz)
    later = after((tb, ta, tz, tokens), o_top, o_low)
    o_right, o_left, o_z, o_own = swap(*later)
    part = sums(ids, halves(1) + [whole(tbz, o_right_z), whole(taz, o_left_z)], [count] * 6)
    part, weights = part[:6], part[6:]
    part = after(part, o_right, o_left, o_z, o_own)
    got = swap(*part[3:])
    far_z, right, left = (add(part[i], got[i]).astype(BF16) for i in range(3))
    far_in, z_right, z_left = move(far_z, zh=1), move(right, dx=1), move(left, dx=-1)

    ids = after(ids, far_z, right, left)
    groups = halves(0) + [whole(tb, o_right), whole(ta, o_left), whole(tz, o_z)]
    part = sums(ids, groups, [h_rows] * 2 + [count] * 3 + [h_rows] * 2 + [count] * 3, weights)
    part, weights = part[:10], part[10:]
    far, near, here_z, near_sib, z_sib = part[:2], part[2:4], part[4], part[7:9], part[9]
    got = swap(*part[5:7])
    far, got, far_in, z_right, z_left = after((far, got, far_in, z_right, z_left))
    top = add(far[0], got[0], far_in[:h_rows]).astype(BF16)
    low = add(far[1], got[1], far_in[h_rows:]).astype(BF16)
    past_top, past_low = move(top, dx=1), move(low, dx=-1)

    near_sib, z_sib = after((near_sib, z_sib), top, low)
    got = swap(*near_sib, z_sib)
    right, left = add(near[0], got[0]), add(near[1], got[1])
    across = add(here_z, got[2], z_right, z_left).astype(BF16)
    ids = after(ids, top, low, right, left, across)
    here, own_sib = sums(ids, [whole(tokens, o_own)], [count] * 2, weights)[:2]
    right, left, across, past_top, past_low, here = after((right, left, across, past_top, past_low, here))
    zero = jnp.zeros((), BF16)
    past_top = lax.pad(past_top, zero, ((0, h_rows, 0), (0, 0, 0)))
    past_low = lax.pad(past_low, zero, ((h_rows, 0, 0), (0, 0, 0)))
    right, left = add(right, past_top).astype(BF16), add(left, past_low).astype(BF16)
    right_in, left_in, across_in = move(right, dx=1), move(left, dx=-1), move(across, zh=1)
    own_sib = after(own_sib, right, left, across)
    base = after(add(here, *swap(own_sib), across_in))
    return add(base, right_in, left_in).astype(BF16)


def solution(mesh):
    return jax.shard_map(
        body,
        mesh=mesh,
        in_specs=(
            P(("dp", "tensor"), None),
            P(("dp", "tensor"), None, None),
            P(("dp", "tensor")),
            P(("dp", "tensor")),
            P(),
            P("tensor", None),
        ),
        out_specs=P(("dp", "tensor"), None),
        check_vma=False,
    )
```

```python
import jax
import jax.numpy as jnp
from jax import lax
from jax.experimental import pallas as pl
from jax.experimental.pallas import tpu as pltpu
from jax.sharding import PartitionSpec as P

NX, NY, NZL, NZH, NC = 4, 4, 2, 2, 2
AXES = ("dp", "tensor")
BF16, F32 = jnp.bfloat16, jnp.float32
NOTE = 16
STEP = 2560


def place(y, zl, zh, x, c):
    return ((y % NY * NZL + zl % NZL) * NZH + zh % NZH) * NX * NC + x % NX * NC + c % NC


def move(value, dx=0, dy=0, zl=0, zh=0, core=0):
    pairs = []
    for y in range(NY):
        for l in range(NZL):
            for h in range(NZH):
                for x in range(NX):
                    for c in range(NC):
                        pairs.append((place(y, l, h, x, c), place(y + dy, l + zl, h + zh, x + dx, c + core)))
    return lax.ppermute(value, AXES, pairs)


def after(value, *others):
    return lax.optimization_barrier((value,) + others)[0]


def rows_of(*parts):
    return jnp.concatenate(parts, axis=0)


def with_note(codes, block_ids, scale_idx):
    _, depth, width = codes.shape

    def kernel(number, entry, block, out, note, sem):
        big = pltpu.make_async_copy(block.at[0], out.at[pl.ds(0, depth)], sem.at[0])
        big.start()
        line = lax.broadcasted_iota(jnp.int32, (NOTE, width), 0)
        note[...] = jnp.where(line == 0, number[0], entry[0]).astype(F32).astype(BF16)
        small = pltpu.make_async_copy(note, out.at[pl.ds(depth, NOTE)], sem.at[1])
        small.start()
        small.wait()
        big.wait()

    smem = pl.BlockSpec(memory_space=pltpu.SMEM)
    anywhere = pl.BlockSpec(memory_space=pltpu.HBM)
    return pl.pallas_call(
        kernel,
        out_shape=jax.ShapeDtypeStruct((depth + NOTE, width), BF16),
        in_specs=[smem, smem, anywhere],
        out_specs=anywhere,
        scratch_shapes=[pltpu.VMEM((NOTE, width), BF16), pltpu.SemaphoreType.DMA((2,))],
        compiler_params=pltpu.CompilerParams(vmem_limit_bytes=2 * 2**20),
    )(block_ids, scale_idx, codes)


def join(pieces, plans):
    n_copies = sum(len(plan) for plan in plans)

    def kernel(*refs):
        sources, outs, sem = refs[: len(pieces)], refs[len(pieces) : -1], refs[-1]
        copies = []
        for plan, out in zip(plans, outs):
            at = 0
            for src, first, n in plan:
                copies.append(
                    pltpu.make_async_copy(sources[src].at[pl.ds(first, n)], out.at[pl.ds(at, n)], sem.at[len(copies)])
                )
                at += n
        for c in copies:
            c.start()
        for c in copies:
            c.wait()

    anywhere = pl.BlockSpec(memory_space=pl.ANY)
    return pl.pallas_call(
        kernel,
        out_shape=tuple(
            jax.ShapeDtypeStruct((sum(n for _, _, n in plan), pieces[plan[0][0]].shape[1]), BF16) for plan in plans
        ),
        in_specs=[anywhere] * len(pieces),
        out_specs=(anywhere,) * len(plans),
        scratch_shapes=[pltpu.SemaphoreType.DMA((n_copies,))],
        compiler_params=pltpu.CompilerParams(vmem_limit_bytes=2 * 2**20),
        cost_estimate=pl.CostEstimate(flops=1, bytes_accessed=1, transcendentals=0),
    )(*pieces)


def feed_forward(code_map, row_map, ranges, depth, width, local_ff, load):
    n_codes = 1 + max(m[1] for m in code_map) if load else 0
    n_rows = 1 + max(m[0] for m in row_map)
    slots = 1 + max(m[0] for m in code_map)
    blocks = slots // 2
    rows = sum(m[2] for m in row_map)
    tile = rows if rows <= 576 else rows // 2
    n_out = len(ranges)
    base = len(code_map) + len(row_map)
    n_copies = base + 1 + 2 * n_out

    def kernel(ids, sidx, table, *refs):
        sources, refs = refs[:n_codes], refs[n_codes:]
        pieces, refs = refs[:n_rows], refs[n_rows:]
        if load:
            down, outs, (w, dn, x, proj, hid, out, sem) = refs[0], refs[1 : 1 + n_out], refs[1 + n_out :]
        else:
            w, dn, outs, (_, _, x, proj, hid, out, sem) = refs[0], refs[1], refs[2 : 2 + n_out], refs[2 + n_out :]
        at = 0
        tiles = [[] for _ in range(rows // tile)]
        for i, (src, start, n) in enumerate(row_map):
            copy = pltpu.make_async_copy(pieces[src].at[pl.ds(start, n)], x.at[pl.ds(at, n)], sem.at[i])
            tiles[at // tile].append(copy)
            at += n
        x_copies = [c for copies in tiles for c in copies]
        if load:
            waits = [[] for _ in range(blocks)]
            for i, (slot, src, start, n, to) in enumerate(code_map):
                target = w.at[slot // 2, pl.ds(to, n), pl.ds(slot % 2 * width, width)]
                waits[slot // 2].append(
                    pltpu.make_async_copy(sources[src].at[pl.ds(start, n)], target, sem.at[len(row_map) + i])
                )
            down_copy = pltpu.make_async_copy(down, dn, sem.at[n_copies - 1])
            stages = [x_copies + waits[0]] + waits[1:] + [[down_copy]]
            for stage in stages[:2]:
                for c in stage:
                    c.start()
        else:
            for c in x_copies:
                c.start()
        for c in tiles[0]:
            c.wait()

        @pl.loop(0, blocks)
        def _(pair):
            if load:
                for q in range(blocks):

                    @pl.when(pair == q)
                    def _(q=q):
                        for c in waits[q]:
                            c.wait()
                        if q + 2 < len(stages):
                            for c in stages[q + 2]:
                                c.start()

            @pl.loop(0, rows // tile)
            def _(part):
                for t in range(1, rows // tile):

                    @pl.when((pair == 0) & (part == t))
                    def _(t=t):
                        for c in tiles[t]:
                            c.wait()

                at = pl.ds(pl.multiple_of(part * tile, tile), tile)
                acc = jnp.dot(x[at, :], w[pair], preferred_element_type=F32)
                for side in range(2):
                    slot = 2 * pair + side
                    proj[ids[slot], at] = acc[:, side * width : (side + 1) * width] * table[sidx[slot]]

        @pl.loop(0, rows // tile)
        def _(part):
            at = pl.ds(pl.multiple_of(part * tile, tile), tile)
            for b in range(blocks):
                gate, up = proj[b, at], proj[b + blocks, at]
                hid[at, b * width : (b + 1) * width] = (gate / (1.0 + jnp.exp(-gate)) * up).astype(BF16)

        if load:
            down_copy.wait()

        def leave(n, slot):
            cols = pl.ds(pl.multiple_of(n * STEP, STEP), STEP)
            return [
                pltpu.make_async_copy(out.at[slot, pl.ds(at, n)], outs[i].at[:, cols], sem.at[base + slot * n_out + i])
                for i, (at, n) in enumerate(ranges)
            ]

        steps = depth // STEP

        @pl.loop(0, steps)
        def _(n):
            slot = lax.rem(n, 2)

            @pl.when(n >= 2)
            def _():
                for c in leave(n - 2, slot):
                    c.wait()

            cols = pl.ds(pl.multiple_of(n * STEP, STEP), STEP)

            @pl.loop(0, rows // tile)
            def _(part):
                at = pl.ds(pl.multiple_of(part * tile, tile), tile)
                out[slot, at] = jnp.dot(hid[at, :], dn[:, cols], preferred_element_type=F32).astype(BF16)

            for c in leave(n, slot):
                c.start()

        for n in (steps - 2, steps - 1):
            for c in leave(n, n % 2):
                c.wait()

    anywhere = pl.BlockSpec(memory_space=pltpu.HBM)
    smem = pl.BlockSpec(memory_space=pltpu.SMEM)
    vmem = pl.BlockSpec(memory_space=pltpu.VMEM)
    results = tuple(jax.ShapeDtypeStruct((n, depth), BF16) for _, n in ranges)
    kept = (pltpu.VMEM((blocks, depth, 2 * width), BF16), pltpu.VMEM((local_ff, depth), BF16))
    return pl.pallas_call(
        kernel,
        out_shape=results + kept,
        in_specs=[smem] * 3 + [anywhere] * (n_codes + n_rows) + ([anywhere] if load else [vmem, vmem]),
        out_specs=(anywhere,) * n_out + (vmem, vmem),
        input_output_aliases={} if load else {3 + n_rows: n_out, 4 + n_rows: n_out + 1},
        scratch_shapes=[
            pltpu.VMEM((rows, depth), BF16),
            pltpu.VMEM((slots, rows, width), F32),
            pltpu.VMEM((rows, local_ff), BF16),
            pltpu.VMEM((2, rows, STEP), BF16),
            pltpu.SemaphoreType.DMA((n_copies,)),
        ],
        compiler_params=pltpu.CompilerParams(vmem_limit_bytes=32 * 2**20),
        cost_estimate=pl.CostEstimate(
            flops=2 * rows * depth * local_ff * 3,
            bytes_accessed=2 * (depth * slots * width + local_ff * depth + 2 * rows * depth),
            transcendentals=rows * local_ff,
        ),
    )


def body(tokens, codes, block_ids, scale_idx, scale_table, down_weight):
    count, depth = tokens.shape
    width = codes.shape[2]
    local_ff = down_weight.shape[0]
    h_rows, h_depth = count // 2, depth // 2

    own = with_note(codes, block_ids, scale_idx)
    ca, cb = move(own, dy=1), move(own, dy=-1)
    ta, tb, tz = move(tokens, dx=1), move(tokens, dx=-1), move(tokens, zh=1)
    cz = move(after(own, tz), zl=1)
    y_top = move(rows_of(ca[:h_depth], ca[depth:]), dy=1)
    y_low = move(cb[h_depth:depth], dy=-1)
    tz_x = after(tz, ta, tb)
    taz, tbz = move(tz_x, dx=1), move(tz_x, dx=-1)
    cy, top_in, low_in = join(
        (y_top, y_low, ta, taz, tb, tbz),
        (
            ((0, 0, h_depth), (1, 0, h_depth), (0, h_depth, NOTE)),
            ((2, 0, h_rows), (3, 0, h_rows)),
            ((4, h_rows, h_rows), (5, h_rows, h_rows)),
        ),
    )
    cy, cz_y = after((cy, cz), top_in)
    caz, cbz, cyz = move(cz_y, dy=1), move(cz_y, dy=-1), move(cy, zl=1)
    x_top, x_low = move(top_in, dx=1), move(low_in, dx=-1)

    sources = [own, ca, cb, cz, cy, caz, cbz, cyz]
    code_map = [(i, i, 0, depth, 0) for i in range(8)]
    notes = jnp.stack([s[depth : depth + 2, 0] for s in sources]).astype(jnp.int32)
    ids, sidx = notes[:, 0], notes[:, 1]

    def swap(*pieces):
        return tuple(move(piece, core=1) for piece in pieces)

    def sums(ids, groups, cuts, weights=None):
        pieces, row_map = [], []
        for piece, first, n in [g[0] for g in groups] + [g[1] for g in groups]:
            held = [i for i, p in enumerate(pieces) if p is piece]
            if not held:
                held = [len(pieces)]
                pieces.append(piece)
            row_map.append((held[0], first, n))
        ranges = [(sum(cuts[:i]), n) for i, n in enumerate(cuts)]
        run = feed_forward(code_map, row_map, ranges, depth, width, local_ff, weights is None)
        if weights is None:
            return tuple(run(ids, sidx, scale_table, *sources, *pieces, down_weight))
        return tuple(run(ids, sidx, scale_table, *pieces, *weights))

    def whole(mine, sibling):
        return (mine, 0, count), (sibling, 0, count)

    def halves(p):
        return [
            ((mine, p * h_rows, h_rows), (sibling, p * h_rows, h_rows))
            for mine, sibling in ((x_top, o_top), (x_low, o_low))
        ]

    def add(*terms):
        total = terms[0].astype(F32)
        for term in terms[1:]:
            total = total + term.astype(F32)
        return total

    o_top, o_low, o_right_z, o_left_z = swap(x_top, x_low, tbz, taz)
    later = after((tb, ta, tz, tokens), o_top, o_low)
    o_right, o_left, o_z, o_own = swap(*later)
    part = sums(ids, halves(1) + [whole(tbz, o_right_z), whole(taz, o_left_z)], [count] * 6)
    part, weights = part[:6], part[6:]
    part = after(part, o_right, o_left, o_z, o_own)
    got = swap(*part[3:])
    far_z, right, left = (add(part[i], got[i]).astype(BF16) for i in range(3))
    far_in, z_right, z_left = move(far_z, zh=1), move(right, dx=1), move(left, dx=-1)

    ids = after(ids, far_z, right, left)
    groups = halves(0) + [whole(tb, o_right), whole(ta, o_left), whole(tz, o_z)]
    part = sums(ids, groups, [h_rows] * 2 + [count] * 3 + [h_rows] * 2 + [count] * 3, weights)
    part, weights = part[:10], part[10:]
    far, near, here_z, near_sib, z_sib = part[:2], part[2:4], part[4], part[7:9], part[9]
    got = swap(*part[5:7])
    far, got, far_in, z_right, z_left = after((far, got, far_in, z_right, z_left))
    top = add(far[0], got[0], far_in[:h_rows]).astype(BF16)
    low = add(far[1], got[1], far_in[h_rows:]).astype(BF16)
    past_top, past_low = move(top, dx=1), move(low, dx=-1)

    near_sib, z_sib = after((near_sib, z_sib), top, low)
    got = swap(*near_sib, z_sib)
    right, left = add(near[0], got[0]), add(near[1], got[1])
    across = add(here_z, got[2], z_right, z_left).astype(BF16)
    ids = after(ids, top, low, right, left, across)
    here, own_sib = sums(ids, [whole(tokens, o_own)], [count] * 2, weights)[:2]
    right, left, across, past_top, past_low, here = after((right, left, across, past_top, past_low, here))
    zero = jnp.zeros((), BF16)
    past_top = lax.pad(past_top, zero, ((0, h_rows, 0), (0, 0, 0)))
    past_low = lax.pad(past_low, zero, ((h_rows, 0, 0), (0, 0, 0)))
    right, left = add(right, past_top).astype(BF16), add(left, past_low).astype(BF16)
    right_in, left_in, across_in = move(right, dx=1), move(left, dx=-1), move(across, zh=1)
    own_sib = after(own_sib, right, left, across)
    base = after(add(here, *swap(own_sib), across_in))
    return add(base, right_in, left_in).astype(BF16)


def solution(mesh):
    return jax.shard_map(
        body,
        mesh=mesh,
        in_specs=(
            P(("dp", "tensor"), None),
            P(("dp", "tensor"), None, None),
            P(("dp", "tensor")),
            P(("dp", "tensor")),
            P(),
            P("tensor", None),
        ),
        out_specs=P(("dp", "tensor"), None),
        check_vma=False,
    )
```
